128 devices in a mesh: seq: 16 (over z, x), chan: 8 (over y, core).
Axes of the slice: x: 4, y: 4, z: 4, core: 2. Of those that a mesh axis runs over, the one named last changes fastest.
Arguments:
- layer_input: bfloat16 [16384, 2048], P(('seq', 'chan')), may hold values from -6 to 6
- kinds: int32 [16384], P('seq'), may hold values from 0 to 2, as said below
- norm_gain: bfloat16 [2048], replicated, may hold values from 0.099609375 to 1.8984375
- in_weight: bfloat16 [3, 2048, 2, 4096], P(None, 'seq', None, 'chan'), may hold values from -0.125 to 0.125
- conv_weight: bfloat16 [4, 4096], P(None, 'chan'), may hold values from -3 to 3
- conv_bias: bfloat16 [4096], P('chan'), may hold values from -3 to 3
- x_weight: bfloat16 [3, 160, 4096], P(None, 'seq', 'chan'), may hold values from -0.09375 to 0.09375
- dt_weight: bfloat16 [3, 128, 4096], P(None, 'seq', 'chan'), may hold values from -0.5 to 0.5
- dt_bias: bfloat16 [4096], P('chan'), may hold values from -6 to -2.5
- a_log: bfloat16 [16, 4096], replicated, may hold values from 0 to 2.765625
- d_skip: bfloat16 [4096], replicated, may hold values from 0.5 to 1.5
- out_weight: bfloat16 [3, 2048, 4096], P(None, 'seq', 'chan'), may hold values from -0.1875 to 0.1875
- cotangent: bfloat16 [16384, 2048], P(('seq', 'chan')), may hold values from -6 to 6
Outputs:
- mixed: bfloat16 [16384, 2048], P(('seq', 'chan'))
- x_grad: float32 [16384, 2048], P(('seq', 'chan'))
- gain_grad: float32 [2048], P(('seq', 'chan'))
- in_grad: float32 [3, 2048, 2, 4096], P(None, 'seq', None, 'chan')
- conv_w_grad: float32 [4, 4096], P(None, ('seq', 'chan'))
- conv_b_grad: float32 [4096], P(('seq', 'chan'))
- x_w_grad: float32 [3, 160, 4096], P(None, 'seq', 'chan')
- dt_w_grad: float32 [3, 128, 4096], P(None, 'seq', 'chan')
- dt_b_grad: float32 [4096], P(('seq', 'chan'))
- a_log_grad: float32 [16, 4096], P(None, ('seq', 'chan'))
- skip_grad: float32 [4096], P(('seq', 'chan'))
- out_grad: float32 [3, 2048, 4096], P(None, 'seq', 'chan')
The draws below stay inside these ranges and needn't reach their ends.
Inputs may be any that keep to these rules, and one draw needn't show every extreme that they name: `kinds`: 0 text, 1 image, 2 other; modalities come in aligned runs of 64 tokens, and a sequence may be text only.
All inputs are finite; a program needn't handle non-finite values.
Results may differ from the reference program's by a relative error of at most 0.012.
The reference program's roundings to bfloat16 on the way count: a program that leaves them out, or rounds other values in their place, can miss the bound.
Values may be sent and summed in bfloat16 or wider, within the bound.
No kernel may reach another device: no remote copies, remote signals or barrier semaphores. Data moves between devices by JAX's collectives and lax.ppermute only.
A program may use at most 256 MiB of HBM per device.

```python
import math
import jax
import jax.numpy as jnp
from jax import lax

D = 2048
E = 4096
NS = 16
KC = 4
R = 128
MODES = 3
RUN = 64
LEN = 1024
TOKENS = 16384
N_SEQ = 16


def draw_kinds(key, part):
    key = jax.random.fold_in(key, 7)
    first_key, second_key = jax.random.split(key)
    sequences = TOKENS // LEN
    text_only = jax.random.randint(first_key, (sequences, 1), 0, 3) == 0
    run_draws = jax.random.randint(second_key, (sequences, LEN // RUN), 0, 8)
    run_kind = jnp.where(run_draws < 4, 0, jnp.where(run_draws < 7, 1, 2))
    run_kind = jnp.where(text_only, 0, run_kind)
    return jnp.repeat(run_kind, RUN, axis=1).reshape(TOKENS).astype(jnp.int32)


def steps_of(key, extent, pieces, least, largest):
    def one(dim, blocks):
        draws = jax.random.uniform(jax.random.fold_in(jax.random.fold_in(key, 6), dim), (blocks,), jnp.float32, least / len(pieces), largest / len(pieces))
        return jnp.repeat(jnp.exp(draws), extent[dim] // blocks).reshape((-1,) + (1,) * (len(extent) - dim - 1))

    factor_of = one(*pieces[0])
    for cut in pieces[1:]:
        factor_of = factor_of * one(*cut)
    return factor_of


def centred(key, dims, spread, reach, pieces=(), dtype=jnp.bfloat16):
    level = steps_of(key, dims, pieces, -0.22, 0.18) if pieces else 1.0
    entries = jax.random.normal(key, dims, jnp.float32) * spread * level
    return jnp.minimum(jnp.maximum(entries, -reach), reach).astype(dtype)


def setup_inputs(seed: int = 0) -> dict:
    key_list = jax.random.split(jax.random.key(seed), 14)
    return {
        "layer_input": centred(key_list[0], (TOKENS, D), 1.0, 6.0, ((0, 128),)),
        "kinds": draw_kinds(jax.random.fold_in(key_list[13], 71), 0),
        "norm_gain": jnp.clip(1.0 + 0.18 * jax.random.normal(key_list[2], (D,), jnp.float32), 0.099609375, 1.8984375).astype(jnp.bfloat16),
        "in_weight": centred(key_list[3], (MODES, D, 2, E), D ** -0.5, 0.125, ((1, 16), (3, 8))),
        "conv_weight": centred(key_list[4], (KC, E), KC ** -0.5, 3.0, ((1, 8),)),
        "conv_bias": centred(key_list[5], (E,), 0.5, 3.0, ((0, 8),)),
        "x_weight": centred(key_list[6], (MODES, R + 2 * NS, E), E ** -0.5, 0.09375, ((1, 16), (2, 8))),
        "dt_weight": centred(key_list[7], (MODES, R, E), R ** -0.5, 0.5, ((1, 16), (2, 8))),
        "dt_bias": jnp.clip(-6.0 + 3.5 * jax.random.uniform(key_list[8], (E,), jnp.float32) ** steps_of(key_list[8], (E,), ((0, 8),), -0.2, 0.2), -6.0, -2.5).astype(jnp.bfloat16),
        "a_log": jnp.clip(jax.random.uniform(key_list[9], (NS, E), jnp.float32, 0.0, 2.765625), 0.0, 2.765625).astype(jnp.bfloat16),
        "d_skip": jnp.clip(jax.random.uniform(key_list[10], (E,), jnp.float32, 0.5, 1.5), 0.5, 1.5).astype(jnp.bfloat16),
        "out_weight": centred(key_list[11], (MODES, D, E), (E // 4) ** -0.5, 0.1875, ((1, 16), (2, 8))),
        "cotangent": centred(key_list[12], (TOKENS, D), 1.0, 6.0, ((0, 128),)),
    }


@jax.custom_vjp
def low(v):
    return lax.optimization_barrier(v.astype(jnp.bfloat16)).astype(jnp.float32)

@jax.custom_vjp
def low_back(v):
    return v

def low_keep(v):
    return (low(v), None)

def low_pass(kept, grad):
    return (grad,)

def back_keep(v):
    return (v, None)

def back_low(kept, grad):
    return (low(grad),)
low.defvjp(low_keep, low_pass)
low_back.defvjp(back_keep, back_low)
highest = lax.Precision.HIGHEST

def token_scan(inputs, deltas, b_input, c_input, decay_rates):
    length = inputs.shape[0]
    stride = math.gcd(length, 32)

    def advance(carried, token_row):
        u_token, dt_token, b_token, c_token = token_row
        carried = jnp.exp(dt_token[None, :] * decay_rates) * carried + b_token[:, None] * (dt_token * u_token)[None, :]
        return (carried, lax.optimization_barrier(jnp.sum(c_token[:, None] * carried, axis=0)))

    @jax.checkpoint
    def run_stride(carried, stride_rows):
        return lax.scan(advance, carried, stride_rows)
    blocked = tuple((member.reshape(length // stride, stride, member.shape[1]) for member in (inputs, deltas, b_input, c_input)))
    initial = jnp.zeros(decay_rates.shape, jnp.float32)
    unused_state, outputs = lax.scan(run_stride, initial, blocked)
    return outputs.reshape(length, inputs.shape[1])

def sequence_layer(tokens, kinds, norm_gain, in_weight, conv_weight, conv_bias, x_weight, dt_weight, dt_bias, a_log, d_skip, out_weight):
    length = tokens.shape[0]
    inverse_rms = lax.rsqrt(lax.optimization_barrier(jnp.mean(tokens * tokens, axis=1, keepdims=True)) + 1e-05)
    normed = low(tokens * inverse_rms * norm_gain)
    masks = [(kinds == mode_index).astype(jnp.float32) for mode_index in range(MODES)]
    joint_proj = jnp.zeros((length, 2, in_weight.shape[3]), jnp.float32)
    for mode_index in range(MODES):
        joint_proj = joint_proj + masks[mode_index][:, None, None] * jnp.einsum('td,dje->tje', normed, in_weight[mode_index], precision=highest)
    joint_proj = low_back(low(joint_proj))
    x_pre = joint_proj[:, 0, :]
    gate_z = joint_proj[:, 1, :]
    padded = jnp.concatenate([jnp.zeros((KC - 1, x_pre.shape[1]), jnp.float32), x_pre], axis=0)
    conv_sum = conv_bias[None, :]
    for tap_index in range(KC):
        conv_sum = conv_sum + conv_weight[tap_index][None, :] * padded[tap_index:tap_index + length]
    u_value = jax.nn.silu(conv_sum)
    u_low = low(u_value)
    projected = jnp.zeros((length, x_weight.shape[1]), jnp.float32)
    for mode_index in range(MODES):
        projected = projected + masks[mode_index][:, None] * jnp.dot(u_low, x_weight[mode_index].T, precision=highest, preferred_element_type=jnp.float32)
    projected = low_back(projected)
    dt_low = low(projected[:, :R])
    b_input = projected[:, R:R + NS]
    c_input = projected[:, R + NS:]
    dt_sum = jnp.zeros((length, dt_weight.shape[2]), jnp.float32)
    for mode_index in range(MODES):
        dt_sum = dt_sum + masks[mode_index][:, None] * jnp.dot(dt_low, dt_weight[mode_index], precision=highest, preferred_element_type=jnp.float32)
    dt_sum = low_back(dt_sum)
    deltas = jax.nn.softplus(dt_sum + dt_bias[None, :])
    decay_rates = -jnp.exp(a_log)
    y_value = token_scan(u_value, deltas, b_input, c_input, decay_rates) + d_skip[None, :] * u_value
    gated = low_back(low(y_value * jax.nn.silu(gate_z)))
    branch = jnp.zeros(tokens.shape, jnp.float32)
    for mode_index in range(MODES):
        branch = branch + masks[mode_index][:, None] * jnp.dot(gated, out_weight[mode_index].T, precision=highest, preferred_element_type=jnp.float32)
    return tokens + branch

def reference(layer_input, kinds, norm_gain, in_weight, conv_weight, conv_bias, x_weight, dt_weight, dt_bias, a_log, d_skip, out_weight, cotangent):
    weights = tuple((member.astype(jnp.float32) for member in (norm_gain, in_weight, conv_weight, conv_bias, x_weight, dt_weight, dt_bias, a_log, d_skip, out_weight)))
    tokens = layer_input.astype(jnp.float32)
    kinds_seq = kinds.reshape(N_SEQ, LEN)

    def whole_layer(token_values, *weight_values):

        def one_sequence(carried, seq_item):
            seq_tokens, seq_kinds = seq_item
            return (carried, jax.checkpoint(sequence_layer)(seq_tokens, seq_kinds, *weight_values))
        unused, outputs = lax.scan(one_sequence, jnp.zeros((), jnp.float32), (token_values.reshape(N_SEQ, LEN, D), kinds_seq))
        return outputs.reshape(TOKENS, D)
    outputs, pullback = jax.vjp(whole_layer, tokens, *weights)
    gradients = pullback(cotangent.astype(jnp.float32))
    return (outputs.astype(jnp.bfloat16), gradients[0], gradients[1], gradients[2], gradients[3], gradients[4], gradients[5], gradients[6], gradients[7], gradients[8], gradients[9], gradients[10])
```

```python
import functools

import jax
import jax.numpy as jnp
from jax import lax
from jax.experimental import pallas as pl
from jax.experimental.pallas import tpu as pltpu
from jax.sharding import Mesh
from jax.sharding import PartitionSpec as P

NS = 16
KC = 4
R = 128
MODES = 3
RUN = 64
RUNS = 16
LEN = 1024
D = 2048
EC = 512
PER = 4
BLK = RUN * PER
NBLK = 6
SLOTS = NBLK * PER
SUB = 16
NSUB = RUN // SUB
LOG2E = 1.4426950408889634
LN2 = 0.6931471805599453
ROWS = MODES * 128
TAIL_IN = 96
TAIL_OUT = 64
PROJ = R + 2 * NS

BF = jnp.bfloat16
F4 = jnp.float32

O_RUN = 0
O_VALID = SLOTS
O_PLACE = 2 * SLOTS
O_BK = 3 * SLOTS
O_TOTAL = O_BK + NBLK
O_KIND = O_TOTAL + 1
O_POS = O_KIND + RUNS

SEQ = ("z", "x")
CHAN = ("y", "c")


def params(limit=56):
    return pltpu.CompilerParams(vmem_limit_bytes=limit << 20)


def cost(flops, moved, trans=0):
    return pl.CostEstimate(flops=int(flops), bytes_accessed=int(moved), transcendentals=int(trans))


def nt(a, b):
    return lax.dot_general(a, b, (((1,), (1,)), ((), ())), preferred_element_type=F4)


def tn(a, b):
    return lax.dot_general(a, b, (((0,), (0,)), ((), ())), preferred_element_type=F4)


def nn(a, b):
    return jnp.dot(a, b, preferred_element_type=F4)


def whole(shape):
    zeros = (0,) * len(shape)
    return pl.BlockSpec(shape, lambda i, pf: zeros)


def slot_plan(kinds):
    me_y, me_c = lax.axis_index("y"), lax.axis_index("c")
    run_kind = kinds.reshape(RUNS, RUN)[:, 0]
    one_hot = (run_kind[:, None] == jnp.arange(MODES, dtype=jnp.int32)[None, :]).astype(jnp.int32)
    count = jnp.sum(one_hot, axis=0)
    blocks = (count + PER - 1) // PER
    first = jnp.cumsum(blocks) - blocks
    rank = jnp.cumsum(one_hot, axis=0) - one_hot
    slot = jnp.sum(one_hot * (PER * first[None, :] + rank), axis=1)
    slots = jnp.arange(SLOTS, dtype=jnp.int32)
    hit = (slot[None, :] == slots[:, None]).astype(jnp.int32)
    valid = jnp.sum(hit, axis=1)
    head = (slot[None, :] == (slots // PER * PER)[:, None]).astype(jnp.int32)
    runs = jnp.arange(RUNS, dtype=jnp.int32)
    run_of = jnp.sum(jnp.where(valid[:, None] > 0, hit, head) * runs[None, :], axis=1)
    total = jnp.sum(blocks)
    place = jnp.minimum(jnp.arange(NBLK, dtype=jnp.int32), total - 1)
    block_kind = jnp.sum((place[:, None] >= first[None, 1:]).astype(jnp.int32), axis=1)

    def position(run):
        core = jnp.where((run // 2) % 2 == me_c, 0, 1)
        return core * 8 + ((run // 4 - me_y) % 4) * 2 + run % 2

    return jnp.concatenate(
        [run_of, valid, position(run_of), block_kind, total[None], run_kind, position(runs)]
    ).astype(jnp.int32)


def slot_run(pf, b, s):
    return pl.multiple_of(pf[O_RUN + b * PER + s] * RUN, RUN)


def slot_place(pf, b, s):
    return pl.multiple_of(pf[O_PLACE + b * PER + s] * RUN, RUN)


def live(i, pf):
    return jnp.minimum(i, pf[O_TOTAL] - 1)


def seq_spec(first):
    return pl.BlockSpec((16, 128, EC), lambda i, pf: (0, first + pf[O_BK + i], 0))


def row_specs():
    def one(s):
        return pl.BlockSpec((RUN, D), lambda i, pf: (pf[O_PLACE + live(i, pf) * PER + s], 0))

    return [one(s) for s in range(PER)]


def down_kernel(pf, x0, x1, x2, x3, w, out):
    b = pl.program_id(0)

    @pl.when(b < pf[O_TOTAL])
    def _():
        rows = jnp.concatenate([x0[...], x1[...], x2[...], x3[...]], axis=0)
        value = nn(rows, w[...].reshape(D, EC)).astype(BF)
        for s in range(PER):
            out[pl.ds(slot_run(pf, b, s), RUN), :] = value[s * RUN : (s + 1) * RUN]


def down(pf, x, w, name, first=0):
    return pl.pallas_call(
        down_kernel,
        out_shape=jax.ShapeDtypeStruct((LEN, EC), BF),
        grid_spec=pltpu.PrefetchScalarGridSpec(
            num_scalar_prefetch=1,
            grid=(NBLK,),
            in_specs=row_specs() + [seq_spec(first)],
            out_specs=whole((LEN, EC)),
        ),
        compiler_params=params(),
        cost_estimate=cost(6 * 2 * BLK * D * EC, 14 << 20),
        name=name,
    )(pf, x, x, x, x, w)


def up_kernel(pf, *refs, pairs, with_gain):
    if with_gain:
        xs = refs[2 * pairs : 2 * pairs + PER]
        near, far, gain, both = refs[2 * pairs + PER :]
    else:
        near, far, both = refs[2 * pairs :]
    b = pl.program_id(0)

    if with_gain:

        @pl.when(b == 0)
        def _():
            gain[...] = jnp.zeros_like(gain)

    @pl.when(b < pf[O_TOTAL])
    def _():
        tile = None
        for p in range(pairs):
            g, w = refs[2 * p], refs[2 * p + 1]
            rows = jnp.concatenate([g[pl.ds(slot_run(pf, b, s), RUN), :] for s in range(PER)], axis=0)
            term = nt(rows, w[...].reshape(D, EC))
            tile = term if p == 0 else tile + term
        for s in range(PER):
            part = tile[s * RUN : (s + 1) * RUN]
            both[pl.ds(slot_place(pf, b, s), RUN), :] = part.astype(BF)
            if with_gain:
                term = jnp.sum(part * xs[s][...].astype(F4), axis=0, keepdims=True)
                gain[...] += jnp.where(pf[O_VALID + b * PER + s] > 0, term, jnp.zeros_like(term))

    @pl.when(b == NBLK - 1)
    def _():
        near[...] = both[: LEN // 2, :]
        far[...] = both[LEN // 2 :, :]


def up(pf, name, *terms, xs=None):
    side = whole((LEN // 2, D))
    args, specs = [], []
    for g, w, first in terms:
        args += [g, w]
        specs += [whole((LEN, EC)), seq_spec(first)]
    out_shape, out_specs = [jax.ShapeDtypeStruct((LEN // 2, D), BF)] * 2, [side] * 2
    if xs is not None:
        args += [xs] * PER
        specs += row_specs()
        out_shape = out_shape + [jax.ShapeDtypeStruct((1, D), F4)]
        out_specs = out_specs + [whole((1, D))]
    return pl.pallas_call(
        functools.partial(up_kernel, pairs=len(terms), with_gain=xs is not None),
        out_shape=out_shape,
        grid_spec=pltpu.PrefetchScalarGridSpec(
            num_scalar_prefetch=1,
            grid=(NBLK,),
            in_specs=specs,
            out_specs=out_specs,
            scratch_shapes=[pltpu.VMEM((LEN, D), BF)],
        ),
        compiler_params=params(),
        cost_estimate=cost(len(terms) * 6 * 2 * BLK * D * EC, 14 << 20),
        name=name,
    )(pf, *args)


def outer_kernel(pf, x_in, g_in, *refs, tail):
    out, acc, sorted_g = refs[-3:]

    @pl.when(pl.program_id(0) == 0)
    def _():
        for b in range(NBLK):
            for s in range(PER):
                rows = g_in[pl.ds(slot_run(pf, b, s), RUN), :]
                rows = jnp.where(pf[O_VALID + b * PER + s] > 0, rows, jnp.zeros_like(rows))
                at = b * BLK + s * RUN
                sorted_g[at : at + RUN, :] = rows

    acc[...] = jnp.zeros_like(acc)
    for b in range(NBLK):

        @pl.when(b < pf[O_TOTAL])
        def _():
            x = jnp.concatenate([x_in[pl.ds(slot_place(pf, b, s), RUN), :] for s in range(PER)], axis=0)
            acc[pf[O_BK + b]] += tn(x, sorted_g[b * BLK : (b + 1) * BLK, :])

    for s in range(4):
        for m in range(MODES):
            out[s, m * 128 : (m + 1) * 128, :] = acc[m, s * 128 : (s + 1) * 128, :].astype(BF)
        if tail:
            dt_tail, x_tail = refs[:2]
            out[s, ROWS:, :] = jnp.concatenate([dt_tail[s], x_tail[s]], axis=0).astype(BF)


def outer(pf, name, x, g, first, held=None, tails=()):
    rows = ROWS + (TAIL_OUT if tails else 0)
    specs = [pl.BlockSpec((LEN, 512), lambda i, pf: (0, i)), whole((LEN, EC))]
    args = [x, g]
    if tails:
        specs += [
            pl.BlockSpec((4, 24, EC), lambda i, pf: (i, 0, 0)),
            pl.BlockSpec((4, TAIL_OUT - 24, EC), lambda i, pf: (i, 0, 0)),
        ]
        args += tails
    aliases = {}
    if held is not None:
        specs.append(pl.BlockSpec(memory_space=pl.ANY))
        args.append(held)
        aliases = {len(args): 0}
    if first % rows == 0:
        out_spec = pl.BlockSpec((4, rows, EC), lambda i, pf: (i, first // rows, 0))
    else:
        out_spec = pl.BlockSpec((pl.Element(4), pl.Element(rows), pl.Element(EC)), lambda i, pf: (4 * i, first, 0))
    return pl.pallas_call(
        functools.partial(outer_kernel, tail=bool(tails)),
        out_shape=jax.ShapeDtypeStruct((16, 3 * ROWS + TAIL_OUT, EC), BF),
        grid_spec=pltpu.PrefetchScalarGridSpec(
            num_scalar_prefetch=1,
            grid=(4,),
            in_specs=specs,
            out_specs=out_spec,
            scratch_shapes=[
                pltpu.VMEM((MODES, 512, EC), F4),
                pltpu.VMEM((NBLK * BLK, EC), BF),
            ],
        ),
        input_output_aliases=aliases,
        compiler_params=params(),
        cost_estimate=cost(6 * 2 * BLK * D * EC, 14 << 20),
        name=name,
    )(pf, *args)


def tail_kernel(pf, target, w, xw, dtw):
    rows = w[...].reshape(16 * TAIL_IN, EC)
    for ref, first in ((xw, 0), (dtw, MODES * PROJ)):
        count = ref.shape[0]
        place = target[first : first + count, :]
        pick = lax.broadcasted_iota(jnp.int32, (count, 16 * TAIL_IN), 1) == place
        ref[...] = nn(jnp.where(pick, 1.0, 0.0).astype(BF), rows).astype(BF)


def tail_rows(pf, w, first):
    i = jnp.arange(MODES * PROJ, dtype=jnp.int32)
    at_x = i % PROJ // 10 * TAIL_IN + i // PROJ * 16 + i % PROJ % 10
    k = jnp.arange(MODES * R, dtype=jnp.int32)
    at_dt = k % R // 8 * TAIL_IN + 48 + k // R * 16 + k % R % 8
    target = jnp.concatenate([at_x, at_dt])[:, None]
    xw, dtw = pl.pallas_call(
        tail_kernel,
        out_shape=[
            jax.ShapeDtypeStruct((MODES * PROJ, EC), BF),
            jax.ShapeDtypeStruct((MODES * R, EC), BF),
        ],
        grid_spec=pltpu.PrefetchScalarGridSpec(
            num_scalar_prefetch=1,
            grid=(1,),
            in_specs=[
                whole((MODES * (PROJ + R), 1)),
                pl.BlockSpec((16, TAIL_IN, EC), lambda i, pf: (0, first // TAIL_IN, 0)),
            ],
            out_specs=[whole((MODES * PROJ, EC)), whole((MODES * R, EC))],
        ),
        compiler_params=params(),
        cost_estimate=cost(1 << 30, 3 << 20),
        name="small_weight_rows",
    )(pf, target, w)
    return xw.reshape(MODES, PROJ, EC), dtw.reshape(MODES, R, EC)


STEPS = 4
ROWS_STEP = LEN // STEPS
SUBS = ROWS_STEP // SUB


def step_spec(width, back=False):
    if back:
        return pl.BlockSpec((ROWS_STEP, width), lambda i, pf: (STEPS - 1 - i, 0))
    return pl.BlockSpec((ROWS_STEP, width), lambda i, pf: (i, 0))


def pos_specs(width, back=False):
    def one(s):
        if back:
            return pl.BlockSpec((RUN, width), lambda i, pf: (pf[O_POS + (STEPS - 1 - i) * PER + s], 0))
        return pl.BlockSpec((RUN, width), lambda i, pf: (pf[O_POS + i * PER + s], 0))

    return [one(s) for s in range(PER)]


def joined(refs):
    return jnp.concatenate([ref[...] for ref in refs], axis=0)


def own_runs(s):
    return slice(s * RUN, (s + 1) * RUN)


def conv_kernel(pf, x, taps, bias, xw, conv_out, part_out, xbuf):
    r = pl.program_id(0)

    @pl.when(r == 0)
    def _():
        xbuf[0:8, :] = jnp.zeros((8, EC), F4)

    @pl.when(r > 0)
    def _():
        xbuf[0:8, :] = xbuf[ROWS_STEP : ROWS_STEP + 8, :]

    xbuf[8:, :] = x[...].astype(F4)
    conv = bias[...] + taps[0:1, :] * xbuf[5 : 5 + ROWS_STEP, :]
    for i in range(1, KC):
        conv = conv + taps[i : i + 1, :] * xbuf[5 + i : 5 + i + ROWS_STEP, :]
    conv_out[...] = conv
    u_low = (conv * jax.nn.sigmoid(conv)).astype(BF)
    for s in range(PER):
        part = nt(u_low[own_runs(s)], xw[pf[O_KIND + r * PER + s]])
        part_out[pl.ds(pl.multiple_of(pf[O_POS + r * PER + s] * RUN, RUN), RUN), :] = part


def conv_call(pf, x_pre, taps, bias, xw):
    return pl.pallas_call(
        conv_kernel,
        out_shape=[
            jax.ShapeDtypeStruct((LEN, EC), F4),
            jax.ShapeDtypeStruct((LEN, PROJ), F4),
        ],
        grid_spec=pltpu.PrefetchScalarGridSpec(
            num_scalar_prefetch=1,
            grid=(STEPS,),
            in_specs=[step_spec(EC), whole((KC, EC)), whole((1, EC)), whole((MODES, PROJ, EC))],
            out_specs=[step_spec(EC), whole((LEN, PROJ))],
            scratch_shapes=[pltpu.VMEM((ROWS_STEP + 8, EC), F4)],
        ),
        compiler_params=params(),
        cost_estimate=cost(1 << 28, 4 << 20, 1 << 20),
        name="conv_project",
    )(pf, x_pre, taps, bias, xw)


def softplus(v):
    return jnp.maximum(v, 0.0) + jnp.log1p(jnp.exp(-jnp.abs(v)))


def halves(v):
    high = v.astype(BF)
    return high, (v - high.astype(F4)).astype(BF)


def masks():
    col = lax.broadcasted_iota(jnp.int32, (ROWS_STEP, SUB * NS), 1)
    row = lax.broadcasted_iota(jnp.int32, (ROWS_STEP, SUB * NS), 0)
    state = lax.broadcasted_iota(jnp.int32, (NS, SUB * NS), 0)
    state_col = lax.broadcasted_iota(jnp.int32, (NS, SUB * NS), 1)
    tiled = jnp.where(state_col % NS == state, 1.0, 0.0).astype(BF)
    return col // NS == row % SUB, tiled


def diagonals(values, own, tiled, out):
    for part, v in enumerate(halves(values)):
        out[part] = jnp.where(own, nn(v, tiled), 0.0).astype(BF).reshape(SUBS, SUB, SUB * NS)


def diagonal(diag, s):
    return jnp.concatenate([diag[0, s], diag[1, s]], axis=0)


def folded(values, own, tiled):
    high, low = halves(jnp.where(own, values, 0.0))
    return nt(high, tiled) + nt(low, tiled)


def columns_of(bct, bc):
    turned = jnp.concatenate([bc, jnp.zeros((ROWS_STEP, 128 - 2 * NS), F4)], axis=1).T
    for s in range(SUBS):
        bct[s] = turned[0 : 2 * NS, s * SUB : (s + 1) * SUB]


def scan_kernel(pf, conv, p0, p1, p2, p3, dtw, dtb, rates, skip, y, v_out, marks, state, dbuf, wbuf, hb0, hb1, bct, diag):
    r = pl.program_id(0)

    @pl.when(r == 0)
    def _():
        state[...] = jnp.zeros_like(state)

    proj = joined((p0, p1, p2, p3))
    low = proj[:, :R].astype(BF)
    v = jnp.concatenate(
        [nn(low[own_runs(s)], dtw[pf[O_KIND + r * PER + s]]) for s in range(PER)], axis=0
    )
    v = v + dtb[...]
    v_out[...] = v
    delta = softplus(v)
    cv = conv[...]
    u = cv * jax.nn.sigmoid(cv)
    dbuf[...] = delta
    wbuf[...] = delta * u
    y[...] = skip[...] * u
    rate = rates[...]
    columns_of(bct, proj[:, R:])
    diagonals(proj[:, R + NS :], *masks(), diag)

    def advance(s, h, hb):
        base = pl.multiple_of(s * SUB, SUB)
        marks[s] = h
        d_rows = dbuf[pl.ds(base, SUB), :]
        w_rows = wbuf[pl.ds(base, SUB), :]
        b_cols = bct[s]
        for i in range(SUB):
            a = jnp.exp2(d_rows[i : i + 1, :] * rate)
            h = a * h + b_cols[0:NS, i : i + 1] * w_rows[i : i + 1, :]
            hb[i * NS : (i + 1) * NS, :] = h.astype(BF)
        return h

    def sums(s, hb):
        both = nn(diagonal(diag, s), hb[...])
        y[pl.ds(pl.multiple_of(s * SUB, SUB), SUB), :] += both[0:SUB] + both[SUB:]

    def pair(k, h):
        sums(2 * k, hb0)
        h = advance(2 * k + 1, h, hb1)
        sums(2 * k + 1, hb1)
        return advance(2 * k + 2, h, hb0)

    h = advance(0, state[...], hb0)
    h = lax.fori_loop(0, SUBS // 2 - 1, pair, h)
    sums(SUBS - 2, hb0)
    state[...] = advance(SUBS - 1, h, hb1)
    sums(SUBS - 1, hb1)


def scan_call(pf, conv, proj, dtw, dtb, rates, skip):
    return pl.pallas_call(
        scan_kernel,
        out_shape=[
            jax.ShapeDtypeStruct((LEN, EC), F4),
            jax.ShapeDtypeStruct((LEN, EC), F4),
            jax.ShapeDtypeStruct((LEN // SUB, NS, EC), F4),
        ],
        grid_spec=pltpu.PrefetchScalarGridSpec(
            num_scalar_prefetch=1,
            grid=(STEPS,),
            in_specs=[step_spec(EC)]
            + pos_specs(PROJ)
            + [whole((MODES, R, EC)), whole((1, EC)), whole((NS, EC)), whole((1, EC))],
            out_specs=[
                step_spec(EC),
                step_spec(EC),
                pl.BlockSpec((SUBS, NS, EC), lambda i, pf: (i, 0, 0)),
            ],
            scratch_shapes=[
                pltpu.VMEM((NS, EC), F4),
                pltpu.VMEM((ROWS_STEP, EC), F4),
                pltpu.VMEM((ROWS_STEP, EC), F4),
                pltpu.VMEM((SUB * NS, EC), BF),
                pltpu.VMEM((SUB * NS, EC), BF),
                pltpu.VMEM((SUBS, 2 * NS, SUB), F4),
                pltpu.VMEM((2, SUBS, SUB, SUB * NS), BF),
            ],
        ),
        compiler_params=params(),
        cost_estimate=cost(1 << 29, 12 << 20, 9 << 20),
        name="scan_forward",
    )(pf, conv, proj, proj, proj, proj, dtw, dtb, rates, skip)


def back_kernel(
    pf, conv, v_in, gg, z, p0, p1, p2, p3, dtw, marks, rates, skip,
    usg, part, dt_tail, alog, dtbg, skipg,
    carry, dtwg, abuf, hprev, hb0, gb0, rb0, hb1, gb1, rb1, dbuf, wbuf, ubuf, ybuf, pbuf, bct, diag, cbuf, bbuf,
):
    r = pl.program_id(0)

    @pl.when(r == 0)
    def _():
        carry[...] = jnp.zeros_like(carry)
        dtwg[...] = jnp.zeros_like(dtwg)
        alog[...] = jnp.zeros_like(alog)
        dtbg[...] = jnp.zeros_like(dtbg)
        skipg[...] = jnp.zeros_like(skipg)

    delta = softplus(v_in[...])
    cv = conv[...]
    u = cv * jax.nn.sigmoid(cv)
    zf = z[...].astype(F4)
    yg = gg[...].astype(F4) * (zf * jax.nn.sigmoid(zf))
    dbuf[...] = delta
    wbuf[...] = delta * u
    ubuf[...] = u
    ybuf[...] = yg
    skipg[...] += jnp.sum(yg * u, axis=0, keepdims=True)
    rate = rates[...]
    proj = joined((p0, p1, p2, p3))
    columns_of(bct, proj[:, R:])
    own, tiled = masks()
    diagonals(proj[:, R : R + NS], own, tiled, diag)

    ones = jnp.where(own[:SUB], 1.0, 0.0).astype(BF)

    def retreat(s, carried, bufs):
        hb, gb, rb = bufs
        ag, al = carried
        base = pl.multiple_of(s * SUB, SUB)
        d_rows = dbuf[pl.ds(base, SUB), :]
        w_rows = wbuf[pl.ds(base, SUB), :]
        y_rows = ybuf[pl.ds(base, SUB), :]
        bc_cols = bct[s]
        h = marks[s]
        for i in range(SUB):
            hprev[i] = h
            a = jnp.exp2(d_rows[i : i + 1, :] * rate)
            abuf[i] = a
            h = a * h + bc_cols[0:NS, i : i + 1] * w_rows[i : i + 1, :]
            hb[i * NS : (i + 1) * NS, :] = h.astype(BF)
        for i in reversed(range(SUB)):
            g = ag + bc_cols[NS:, i : i + 1] * y_rows[i : i + 1, :]
            gb[i * NS : (i + 1) * NS, :] = g.astype(BF)
            ag = abuf[i] * g
            rp = rate * (ag * hprev[i])
            rb[i * NS : (i + 1) * NS, :] = rp.astype(BF)
            al = al + d_rows[i : i + 1, :] * rp
        return ag, al

    def sums(s, bufs):
        hb, gb, rb = bufs
        at = pl.ds(pl.multiple_of(s * SUB, SUB), SUB)
        both = nn(diagonal(diag, s), gb[...])
        bsum = both[0:SUB] + both[SUB:]
        dsum = nn(ones, rb[...])
        cbuf[at, :] = nt(ybuf[at, :].astype(BF), hb[...])
        bbuf[at, :] = nt(wbuf[at, :].astype(BF), gb[...])
        usg[at, :] = dbuf[at, :] * bsum + skip[...] * ybuf[at, :]
        pbuf[at, :] = dsum * LN2 + ubuf[at, :] * bsum

    even, odd = (hb0, gb0, rb0), (hb1, gb1, rb1)

    def pair(k, carried):
        s = SUBS - 1 - 2 * k
        sums(s, even)
        carried = retreat(s - 1, carried, odd)
        sums(s - 1, odd)
        return retreat(s - 2, carried, even)

    carried = retreat(SUBS - 1, (carry[...], jnp.zeros((NS, EC), F4)), even)
    carried = lax.fori_loop(0, SUBS // 2 - 1, pair, carried)
    sums(1, even)
    ag, al = retreat(0, carried, odd)
    sums(0, odd)
    carry[...] = ag
    alog[...] += al * LN2
    pre = pbuf[...] * jax.nn.sigmoid(v_in[...])
    dtbg[...] += jnp.sum(pre, axis=0, keepdims=True)
    pre_low = pre.astype(BF)
    bgrad = folded(bbuf[...], own, tiled)
    cgrad = folded(cbuf[...], own, tiled)
    low = proj[:, :R].astype(BF)
    for s in range(PER):
        run = (STEPS - 1 - r) * PER + s
        kind = pf[O_KIND + run]
        at = pl.ds(pl.multiple_of(pf[O_POS + run] * RUN, RUN), RUN)
        part[at, :R] = nt(pre_low[own_runs(s)], dtw[kind])
        part[at, R : R + NS] = bgrad[own_runs(s)]
        part[at, R + NS :] = cgrad[own_runs(s)]
        dtwg[kind] += tn(low[own_runs(s)], pre_low[own_runs(s)])

    @pl.when(r == STEPS - 1)
    def _():
        for s in range(16):
            for m in range(MODES):
                dt_tail[s, m * 8 : (m + 1) * 8, :] = dtwg[m, s * 8 : (s + 1) * 8, :]


def back_call(pf, conv, v, gg, z, proj, dtw, marks, rates, skip):
    return pl.pallas_call(
        back_kernel,
        out_shape=[
            jax.ShapeDtypeStruct((LEN, EC), F4),
            jax.ShapeDtypeStruct((LEN, PROJ), F4),
            jax.ShapeDtypeStruct((16, MODES * 8, EC), F4),
            jax.ShapeDtypeStruct((NS, EC), F4),
            jax.ShapeDtypeStruct((1, EC), F4),
            jax.ShapeDtypeStruct((1, EC), F4),
        ],
        grid_spec=pltpu.PrefetchScalarGridSpec(
            num_scalar_prefetch=1,
            grid=(STEPS,),
            in_specs=[step_spec(EC, True)] * 4
            + pos_specs(PROJ, True)
            + [
                whole((MODES, R, EC)),
                pl.BlockSpec((SUBS, NS, EC), lambda i, pf: (STEPS - 1 - i, 0, 0)),
                whole((NS, EC)),
                whole((1, EC)),
            ],
            out_specs=[
                step_spec(EC, True),
                whole((LEN, PROJ)),
                whole((16, MODES * 8, EC)),
                whole((NS, EC)),
                whole((1, EC)),
                whole((1, EC)),
            ],
            scratch_shapes=[
                pltpu.VMEM((NS, EC), F4),
                pltpu.VMEM((MODES, R, EC), F4),
                pltpu.VMEM((SUB, NS, EC), F4),
                pltpu.VMEM((SUB, NS, EC), F4),
                *[pltpu.VMEM((SUB * NS, EC), BF)] * 6,
                pltpu.VMEM((ROWS_STEP, EC), F4),
                pltpu.VMEM((ROWS_STEP, EC), F4),
                pltpu.VMEM((ROWS_STEP, EC), F4),
                pltpu.VMEM((ROWS_STEP, EC), F4),
                pltpu.VMEM((ROWS_STEP, EC), F4),
                pltpu.VMEM((SUBS, 2 * NS, SUB), F4),
                pltpu.VMEM((2, SUBS, SUB, SUB * NS), BF),
                pltpu.VMEM((ROWS_STEP, SUB * NS), F4),
                pltpu.VMEM((ROWS_STEP, SUB * NS), F4),
            ],
        ),
        compiler_params=params(),
        cost_estimate=cost(1 << 30, 14 << 20, 9 << 20),
        name="scan_backward",
    )(pf, conv, v, gg, z, proj, proj, proj, proj, dtw, marks, rates, skip)


def conv_back_kernel(
    pf, p0, p1, p2, p3, xw, usg, conv, x_now, x_before, taps,
    out, x_tail, cwg, cbg, gbuf, xbuf, xwg,
):
    r = pl.program_id(0)

    @pl.when(r == 0)
    def _():
        xwg[...] = jnp.zeros_like(xwg)
        cwg[...] = jnp.zeros_like(cwg)
        cbg[...] = jnp.zeros_like(cbg)
        gbuf[ROWS_STEP:, :] = jnp.zeros((8, EC), F4)

    @pl.when(r > 0)
    def _():
        gbuf[ROWS_STEP:, :] = gbuf[0:8, :]

    cv = conv[...]
    q = jax.nn.sigmoid(cv)
    u_low = (cv * q).astype(BF)
    pgs = (p0, p1, p2, p3)
    kinds = [pf[O_KIND + (STEPS - 1 - r) * PER + s] for s in range(PER)]
    u_grad = usg[...] + jnp.concatenate([nn(pgs[s][...], xw[kinds[s]]) for s in range(PER)], axis=0)
    grad = u_grad * (q * (1.0 + cv * (1.0 - q)))
    gbuf[0:ROWS_STEP, :] = grad
    cbg[...] += jnp.sum(grad, axis=0, keepdims=True)
    before = x_before[...].astype(F4)[16 - 8 :, :]
    xbuf[0:8, :] = jnp.where(r == STEPS - 1, jnp.zeros_like(before), before)
    xbuf[8:, :] = x_now[...].astype(F4)
    back = taps[KC - 1 : KC, :] * grad
    for i in range(KC):
        cwg[i : i + 1, :] += jnp.sum(grad * xbuf[5 + i : 5 + i + ROWS_STEP, :], axis=0, keepdims=True)
        if i < KC - 1:
            back = back + taps[i : i + 1, :] * gbuf[KC - 1 - i : KC - 1 - i + ROWS_STEP, :]
    out[...] = back.astype(BF)
    for s in range(PER):
        xwg[kinds[s]] += tn(pgs[s][...], u_low[own_runs(s)])

    @pl.when(r == STEPS - 1)
    def _():
        for s in range(16):
            for m in range(MODES):
                x_tail[s, m * 10 : (m + 1) * 10, :] = xwg[m, s * 10 : (s + 1) * 10, :]
            x_tail[s, MODES * 10 :, :] = jnp.zeros((TAIL_OUT - 24 - MODES * 10, EC), F4)


def conv_back_call(pf, pg, xw, usg, conv, x_pre, taps):
    before = ROWS_STEP // 16
    return pl.pallas_call(
        conv_back_kernel,
        out_shape=[
            jax.ShapeDtypeStruct((LEN, EC), BF),
            jax.ShapeDtypeStruct((16, TAIL_OUT - 24, EC), F4),
            jax.ShapeDtypeStruct((KC, EC), F4),
            jax.ShapeDtypeStruct((1, EC), F4),
        ],
        grid_spec=pltpu.PrefetchScalarGridSpec(
            num_scalar_prefetch=1,
            grid=(STEPS,),
            in_specs=pos_specs(PROJ, True)
            + [
                whole((MODES, PROJ, EC)),
                step_spec(EC, True),
                step_spec(EC, True),
                step_spec(EC, True),
                pl.BlockSpec(
                    (16, EC), lambda i, pf: (jnp.maximum((STEPS - 1 - i) * before - 1, 0), 0)
                ),
                whole((KC, EC)),
            ],
            out_specs=[
                step_spec(EC, True),
                whole((16, TAIL_OUT - 24, EC)),
                whole((KC, EC)),
                whole((1, EC)),
            ],
            scratch_shapes=[
                pltpu.VMEM((ROWS_STEP + 8, EC), F4),
                pltpu.VMEM((ROWS_STEP + 8, EC), F4),
                pltpu.VMEM((MODES, PROJ, EC), F4),
            ],
        ),
        compiler_params=params(),
        cost_estimate=cost(1 << 29, 8 << 20, 1 << 20),
        name="conv_backward",
    )(pf, pg, pg, pg, pg, xw, usg, conv, x_pre, x_pre, taps)


def ring(v, axis, step):
    return lax.ppermute(v, axis, [(i, (i + step) % 4) for i in range(4)])


def across(v):
    return lax.ppermute(v, "c", [(0, 1), (1, 0)])


def after(value, *others):
    return lax.optimization_barrier((value, others))[0]


def add(*values):
    total = values[0].astype(F4)
    for value in values[1:]:
        total = total + value.astype(F4)
    return total


def spread_chan(rows):
    left = ring(rows, "y", 1)
    right = ring(rows, "y", -1)
    far = [ring(left[:RUN], "y", 1), ring(right[RUN:], "y", -1)]
    near = jnp.concatenate([rows, right, *far, left], axis=0)
    return jnp.concatenate([near, across(near)], axis=0)


def collect_chan(near, far):
    pair = add(near, across(far)).astype(BF).reshape(4, 2 * RUN, D)
    own, right, far_first, far_second, left = pair[0], pair[1], pair[2, :RUN], pair[2, RUN:], pair[3]
    came = ring(far_first, "y", 1)
    came_back = ring(far_second, "y", -1)
    right = jnp.concatenate([add(right[:RUN], came).astype(BF), right[RUN:]], axis=0)
    left = jnp.concatenate([left[:RUN], add(left[RUN:], came_back).astype(BF)], axis=0)
    return add(own, ring(right, "y", 1), ring(left, "y", -1))


def direct(v, axis):
    return [v, ring(v, axis, -1), ring(v, axis, 2), ring(v, axis, 1)]


def sum_chan(part, finish, fill=None, fill_more=None):
    half = LEN // 2
    pair = add(part[:half], across(part[half:])).reshape(4, half // 4, part.shape[1])
    came = [ring(pair[1], "y", 1), ring(pair[2], "y", 2), ring(pair[3], "y", -1)]
    filled = None
    if fill:
        filled = fill(pair)
        came = after(came, filled)
    total = finish(add(pair[0], *came))
    lines = direct(total, "y")
    if fill_more:
        filled = fill_more(total, filled)
        lines = after(lines, filled)
    mine = jnp.concatenate(lines, axis=0)
    return jnp.concatenate([mine, across(mine)], axis=0), filled


def sum_axis(v, axis):
    v = jnp.roll(v, -lax.axis_index(axis), 0)
    return add(v[0], ring(v[1], axis, 1), ring(v[2], axis, 2), ring(v[3], axis, -1))


def sum_pair(v):
    place = lax.axis_index("c")
    keep = lax.dynamic_index_in_dim(v, place, 2, False)
    give = lax.dynamic_index_in_dim(v, 1 - place, 2, False)
    return sum_axis(jnp.swapaxes(keep + across(give), 0, 1), "y")


def sum_seq(v):
    return sum_axis(sum_axis(v.reshape(4, 4, v.shape[1]), "z"), "x")


def local(
    layer_input, kinds, norm_gain, in_weight, conv_weight, conv_bias, x_weight, dt_weight,
    dt_bias, a_log, d_skip, out_weight, cotangent,
):
    place_y, place_c = lax.axis_index("y"), lax.axis_index("c")
    chan = place_y * 2 + place_c
    gain = norm_gain.astype(F4)
    taps = conv_weight.astype(F4)
    cbias = conv_bias.astype(F4)[None, :]
    dtb = dt_bias.astype(F4)[None, :]
    a_own = lax.dynamic_slice_in_dim(a_log, chan * EC, EC, 1).astype(F4)
    rates = -jnp.exp(a_own) * LOG2E
    skip = lax.dynamic_slice_in_dim(d_skip, chan * EC, EC, 0).astype(F4)[None, :]

    x32 = layer_input.astype(F4)
    rms = lax.rsqrt(jnp.mean(x32 * x32, axis=1, keepdims=True) + 1e-05)
    normed = (x32 * rms * gain[None, :]).astype(BF)

    early_w = lax.all_gather(
        jnp.concatenate(
            [
                in_weight[:, :, 0, :].reshape(ROWS, EC),
                in_weight[:, :, 1, :].reshape(ROWS, EC),
                jnp.pad(x_weight, ((0, 0), (0, 6), (0, 0))).reshape(48, EC),
                jnp.pad(dt_weight, ((0, 0), (0, 8), (0, 0))).reshape(48, EC),
            ],
            axis=0,
        ),
        SEQ,
    )
    pf = slot_plan(kinds)
    xs = spread_chan(normed)
    cs = spread_chan(cotangent)
    out_w = lax.all_gather(after(out_weight.reshape(ROWS, EC), xs, cs), SEQ)
    rates, skip, taps, cbias, dtb, xs = after((rates, skip, taps, cbias, dtb, xs), pf)
    early_w = after(early_w, rates, skip, taps, cbias, dtb, xs)
    x_pre = down(pf, xs, early_w, "project_scan")
    xw, dtw = tail_rows(pf, early_w, 2 * ROWS)
    conv, part = conv_call(pf, x_pre, taps, cbias, xw)
    proj, _ = sum_chan(part, lambda total: total)
    y, v, marks = scan_call(pf, conv, proj, dtw, dtb, rates, skip)

    z = down(pf, xs, early_w, "project_gate", MODES)
    z32 = z.astype(F4)
    q = jax.nn.sigmoid(z32)
    gated = (y * (z32 * q)).astype(BF)
    weights_part = outer(pf, "out_weight_grad", cs, gated, 0)
    gg = down(pf, after(cs, weights_part), out_w, "project_cotangent")
    zgrad = (gg.astype(F4) * y * (q * (1.0 + z32 * (1.0 - q)))).astype(BF)

    usg, proj_part, dt_tail, alog, dtbg, skipg = back_call(
        pf, conv, v, gg, z, proj, dtw, marks, rates, skip
    )
    pg, weights_part = sum_chan(
        proj_part,
        lambda total: total.astype(BF),
        lambda pair: outer(pf, "gate_weight_grad", xs, after(zgrad, pair), ROWS, weights_part),
    )
    xgrad, x_tail, cwg, cbg = conv_back_call(pf, pg, xw, usg, conv, x_pre, taps)
    weights_part = outer(
        pf, "scan_weight_grad", xs, xgrad, 2 * ROWS, weights_part, (dt_tail, x_tail)
    )
    weights_sum = lax.psum_scatter(weights_part, SEQ, scatter_dimension=0).astype(F4)

    zgrad, gated = after((zgrad, gated), weights_part)
    branch = collect_chan(*up(pf, "project_out", (gated, out_w, 0)))
    mixed = (x32 + branch).astype(BF)
    near, far, gain_part = up(
        pf, "input_grad", (xgrad, early_w, 0), (zgrad, early_w, MODES), xs=xs
    )
    ngrad = collect_chan(near, far) * gain[None, :]
    x_grad = (
        cotangent.astype(F4)
        + rms * ngrad
        - x32 * (rms * rms * rms) * jnp.mean(ngrad * x32, axis=1, keepdims=True)
    )
    in_grad = jnp.stack(
        [
            weights_sum[2 * ROWS : 3 * ROWS].reshape(MODES, 128, EC),
            weights_sum[ROWS : 2 * ROWS].reshape(MODES, 128, EC),
        ],
        axis=2,
    )
    out_grad = weights_sum[:ROWS].reshape(MODES, 128, EC)
    dt_w_grad = weights_sum[3 * ROWS : 3 * ROWS + 24].reshape(MODES, 8, EC)
    x_w_grad = weights_sum[3 * ROWS + 24 : 3 * ROWS + 54].reshape(MODES, 10, EC)
    gain_part = sum_pair((gain_part[0] / gain).reshape(16, 4, 2, 16))
    small = jnp.concatenate([cwg, cbg, dtbg, skipg, alog], axis=0)
    small = jnp.swapaxes(small.reshape(23, 16, 32), 0, 1).reshape(16, 23 * 32)
    small = sum_seq(jnp.concatenate([small, gain_part, jnp.zeros((16, 16), F4)], axis=1))
    gain_grad = small[23 * 32 : 24 * 32 - 16]
    moves = [(s * 8 + c, c * 16 + s) for s in range(16) for c in range(8)]
    own = lax.ppermute(small[: 23 * 32].reshape(23, 32), ("z", "x", "y", "c"), moves)
    return (
        mixed,
        x_grad,
        gain_grad,
        in_grad,
        own[0:4],
        own[4],
        x_w_grad,
        dt_w_grad,
        own[5],
        own[7:],
        own[6],
        out_grad,
    )


def solution(mesh):
    fine = Mesh(mesh.devices.reshape(4, 4, 4, 2), ("z", "x", "y", "c"))
    rows = ("z", "x", "y", "c")
    return jax.shard_map(
        local,
        mesh=fine,
        in_specs=(
            P(rows, None),
            P(SEQ),
            P(),
            P(None, SEQ, None, CHAN),
            P(None, CHAN),
            P(CHAN),
            P(None, SEQ, CHAN),
            P(None, SEQ, CHAN),
            P(CHAN),
            P(),
            P(),
            P(None, SEQ, CHAN),
            P(rows, None),
        ),
        out_specs=(
            P(rows, None),
            P(rows, None),
            P(rows),
            P(None, SEQ, None, CHAN),
            P(None, rows),
            P(rows),
            P(None, SEQ, CHAN),
            P(None, SEQ, CHAN),
            P(rows),
            P(None, rows),
            P(rows),
            P(None, SEQ, CHAN),
        ),
        check_vma=False,
    )
```

```python
import functools

import jax
import jax.numpy as jnp
import numpy as np
from jax import lax
from jax.experimental import pallas as pl
from jax.experimental.pallas import tpu as pltpu
from jax.sharding import Mesh
from jax.sharding import PartitionSpec as P

NS = 16
KC = 4
R = 128
MODES = 3
RUN = 64
RUNS = 16
LEN = 1024
D = 2048
EC = 512
PER = 4
BLK = RUN * PER
NBLK = 6
SLOTS = NBLK * PER
SUB = 16
NSUB = RUN // SUB
LOG2E = 1.4426950408889634
LN2 = 0.6931471805599453
ROWS = MODES * 128
TAIL_IN = 96
TAIL_OUT = 64
PROJ = R + 2 * NS

BF = jnp.bfloat16
F4 = jnp.float32

O_RUN = 0
O_VALID = SLOTS
O_PLACE = 2 * SLOTS
O_BK = 3 * SLOTS
O_TOTAL = O_BK + NBLK
O_KIND = O_TOTAL + 1
O_POS = O_KIND + RUNS

SEQ = ("z", "x")
CHAN = ("y", "c")


def params(limit=56):
    return pltpu.CompilerParams(vmem_limit_bytes=limit << 20)


def in_hbm(x):
    return pltpu.with_memory_space_constraint(x, pltpu.HBM)


def cost(flops, moved, trans=0):
    return pl.CostEstimate(flops=int(flops), bytes_accessed=int(moved), transcendentals=int(trans))


def nt(a, b):
    return lax.dot_general(a, b, (((1,), (1,)), ((), ())), preferred_element_type=F4)


def tn(a, b):
    return lax.dot_general(a, b, (((0,), (0,)), ((), ())), preferred_element_type=F4)


def nn(a, b):
    return jnp.dot(a, b, preferred_element_type=F4)


def whole(shape):
    zeros = (0,) * len(shape)
    return pl.BlockSpec(shape, lambda i, pf: zeros)


def slot_plan(kinds):
    me_y, me_c = lax.axis_index("y"), lax.axis_index("c")
    run_kind = kinds.reshape(RUNS, RUN)[:, 0]
    one_hot = (run_kind[:, None] == jnp.arange(MODES, dtype=jnp.int32)[None, :]).astype(jnp.int32)
    count = jnp.sum(one_hot, axis=0)
    blocks = (count + PER - 1) // PER
    first = jnp.cumsum(blocks) - blocks
    rank = jnp.cumsum(one_hot, axis=0) - one_hot
    slot = jnp.sum(one_hot * (PER * first[None, :] + rank), axis=1)
    slots = jnp.arange(SLOTS, dtype=jnp.int32)
    hit = (slot[None, :] == slots[:, None]).astype(jnp.int32)
    valid = jnp.sum(hit, axis=1)
    head = (slot[None, :] == (slots // PER * PER)[:, None]).astype(jnp.int32)
    runs = jnp.arange(RUNS, dtype=jnp.int32)
    run_of = jnp.sum(jnp.where(valid[:, None] > 0, hit, head) * runs[None, :], axis=1)
    total = jnp.sum(blocks)
    place = jnp.minimum(jnp.arange(NBLK, dtype=jnp.int32), total - 1)
    block_kind = jnp.sum((place[:, None] >= first[None, 1:]).astype(jnp.int32), axis=1)

    def position(run):
        core = jnp.where((run // 2) % 2 == me_c, 0, 1)
        return core * 8 + ((run // 4 - me_y) % 4) * 2 + run % 2

    return jnp.concatenate(
        [run_of, valid, position(run_of), block_kind, total[None], run_kind, position(runs)]
    ).astype(jnp.int32)


def slot_run(pf, b, s):
    return pl.multiple_of(pf[O_RUN + b * PER + s] * RUN, RUN)


def slot_place(pf, b, s):
    return pl.multiple_of(pf[O_PLACE + b * PER + s] * RUN, RUN)


def live(i, pf):
    return jnp.minimum(i, pf[O_TOTAL] - 1)


def seq_spec(first):
    return pl.BlockSpec((16, 128, EC), lambda i, pf: (0, first + pf[O_BK + i], 0))


def row_specs():
    def one(s):
        return pl.BlockSpec((RUN, D), lambda i, pf: (pf[O_PLACE + live(i, pf) * PER + s], 0))

    return [one(s) for s in range(PER)]


def down_kernel(pf, x0, x1, x2, x3, w, out):
    b = pl.program_id(0)

    @pl.when(b < pf[O_TOTAL])
    def _():
        rows = jnp.concatenate([x0[...], x1[...], x2[...], x3[...]], axis=0)
        value = nn(rows, w[...].reshape(D, EC)).astype(BF)
        for s in range(PER):
            out[pl.ds(slot_run(pf, b, s), RUN), :] = value[s * RUN : (s + 1) * RUN]


def down(pf, x, w, name, first=0):
    return pl.pallas_call(
        down_kernel,
        out_shape=jax.ShapeDtypeStruct((LEN, EC), BF),
        grid_spec=pltpu.PrefetchScalarGridSpec(
            num_scalar_prefetch=1,
            grid=(NBLK,),
            in_specs=row_specs() + [seq_spec(first)],
            out_specs=whole((LEN, EC)),
        ),
        compiler_params=params(16),
        cost_estimate=cost(6 * 2 * BLK * D * EC, 14 << 20),
        name=name,
    )(pf, x, x, x, x, in_hbm(w))


def up_kernel(pf, *refs, pairs, with_gain):
    if with_gain:
        xs = refs[2 * pairs : 2 * pairs + PER]
        near, far, gain, both = refs[2 * pairs + PER :]
    else:
        near, far, both = refs[2 * pairs :]
    b = pl.program_id(0)

    if with_gain:

        @pl.when(b == 0)
        def _():
            gain[...] = jnp.zeros_like(gain)

    @pl.when(b < pf[O_TOTAL])
    def _():
        tile = None
        for p in range(pairs):
            g, w = refs[2 * p], refs[2 * p + 1]
            rows = jnp.concatenate([g[pl.ds(slot_run(pf, b, s), RUN), :] for s in range(PER)], axis=0)
            term = nt(rows, w[...].reshape(D, EC))
            tile = term if p == 0 else tile + term
        for s in range(PER):
            part = tile[s * RUN : (s + 1) * RUN]
            both[pl.ds(slot_place(pf, b, s), RUN), :] = part.astype(BF)
            if with_gain:
                term = jnp.sum(part * xs[s][...].astype(F4), axis=0, keepdims=True)
                gain[...] += jnp.where(pf[O_VALID + b * PER + s] > 0, term, jnp.zeros_like(term))

    @pl.when(b == NBLK - 1)
    def _():
        near[...] = both[: LEN // 2, :]
        far[...] = both[LEN // 2 :, :]


def up(pf, name, *terms, xs=None):
    side = whole((LEN // 2, D))
    args, specs = [], []
    for g, w, first in terms:
        args += [g, in_hbm(w)]
        specs += [whole((LEN, EC)), seq_spec(first)]
    out_shape, out_specs = [pltpu.HBM((LEN // 2, D), BF)] * 2, [side] * 2
    if xs is not None:
        args += [xs] * PER
        specs += row_specs()
        out_shape = out_shape + [jax.ShapeDtypeStruct((1, D), F4)]
        out_specs = out_specs + [whole((1, D))]
    return pl.pallas_call(
        functools.partial(up_kernel, pairs=len(terms), with_gain=xs is not None),
        out_shape=out_shape,
        grid_spec=pltpu.PrefetchScalarGridSpec(
            num_scalar_prefetch=1,
            grid=(NBLK,),
            in_specs=specs,
            out_specs=out_specs,
            scratch_shapes=[pltpu.VMEM((LEN, D), BF)],
        ),
        compiler_params=params(32),
        cost_estimate=cost(len(terms) * 6 * 2 * BLK * D * EC, 14 << 20),
        name=name,
    )(pf, *args)


def outer_kernel(pf, x_in, g_in, *refs, tail):
    out, acc, sorted_g = refs[-3:]

    @pl.when(pl.program_id(0) == 0)
    def _():
        for b in range(NBLK):
            for s in range(PER):
                rows = g_in[pl.ds(slot_run(pf, b, s), RUN), :]
                rows = jnp.where(pf[O_VALID + b * PER + s] > 0, rows, jnp.zeros_like(rows))
                at = b * BLK + s * RUN
                sorted_g[at : at + RUN, :] = rows

    acc[...] = jnp.zeros_like(acc)
    for b in range(NBLK):

        @pl.when(b < pf[O_TOTAL])
        def _():
            x = jnp.concatenate([x_in[pl.ds(slot_place(pf, b, s), RUN), :] for s in range(PER)], axis=0)
            acc[pf[O_BK + b]] += tn(x, sorted_g[b * BLK : (b + 1) * BLK, :])

    for s in range(4):
        for m in range(MODES):
            out[s, m * 128 : (m + 1) * 128, :] = acc[m, s * 128 : (s + 1) * 128, :].astype(BF)
        if tail:
            dt_tail, x_tail = refs[:2]
            out[s, ROWS:, :] = jnp.concatenate([dt_tail[s], x_tail[s]], axis=0).astype(BF)


def outer(pf, name, x, g, held_rows, first=0, held=None, tails=()):
    rows = ROWS + (TAIL_OUT if tails else 0)
    specs = [pl.BlockSpec((LEN, 512), lambda i, pf: (0, i)), whole((LEN, EC))]
    args = [x, g]
    if tails:
        specs += [
            pl.BlockSpec((4, 24, EC), lambda i, pf: (i, 0, 0)),
            pl.BlockSpec((4, TAIL_OUT - 24, EC), lambda i, pf: (i, 0, 0)),
        ]
        args += tails
    aliases = {}
    if held is not None:
        specs.append(pl.BlockSpec(memory_space=pl.ANY))
        args.append(held)
        aliases = {len(args): 0}
    if first % rows == 0:
        out_spec = pl.BlockSpec((4, rows, EC), lambda i, pf: (i, first // rows, 0))
    else:
        out_spec = pl.BlockSpec((pl.Element(4), pl.Element(rows), pl.Element(EC)), lambda i, pf: (4 * i, first, 0))
    return pl.pallas_call(
        functools.partial(outer_kernel, tail=bool(tails)),
        out_shape=pltpu.HBM((16, held_rows, EC), BF),
        grid_spec=pltpu.PrefetchScalarGridSpec(
            num_scalar_prefetch=1,
            grid=(4,),
            in_specs=specs,
            out_specs=out_spec,
            scratch_shapes=[
                pltpu.VMEM((MODES, 512, EC), F4),
                pltpu.VMEM((NBLK * BLK, EC), BF),
            ],
        ),
        input_output_aliases=aliases,
        compiler_params=params(20),
        cost_estimate=cost(6 * 2 * BLK * D * EC, 14 << 20),
        name=name,
    )(pf, *args)


def picker(count, rows):
    i = np.arange(count)
    return jnp.asarray(np.arange(256)[None, :] == (i // rows * 16 + i % rows)[:, None], BF)


STEPS = 4
PER_STEP = RUNS // STEPS
ROWS_STEP = LEN // STEPS
SUBS = ROWS_STEP // SUB


def step_spec(width, back=False):
    if back:
        return pl.BlockSpec((ROWS_STEP, width), lambda i, pf: (STEPS - 1 - i, 0))
    return pl.BlockSpec((ROWS_STEP, width), lambda i, pf: (i, 0))


def pos_specs(width, back=False):
    def one(s):
        if back:
            return pl.BlockSpec((RUN, width), lambda i, pf: (pf[O_POS + (STEPS - 1 - i) * PER_STEP + s], 0))
        return pl.BlockSpec((RUN, width), lambda i, pf: (pf[O_POS + i * PER_STEP + s], 0))

    return [one(s) for s in range(PER_STEP)]


def joined(refs):
    return jnp.concatenate([ref[...] for ref in refs], axis=0)


def own_runs(s):
    return slice(s * RUN, (s + 1) * RUN)


def conv_kernel(pf, x, taps, bias, pick_x, pick_dt, w, u_out, slope_out, near, far, xw, dtw, xbuf, part_out):
    r = pl.program_id(0)

    @pl.when(r == 0)
    def _():
        for m in range(MODES):
            for ref, pick, first in ((xw, pick_x, 0), (dtw, pick_dt, 48)):
                rows = w[:, first + m * 16 : first + (m + 1) * 16, :].reshape(256, EC)
                ref[m] = nn(pick[...], rows).astype(BF)
        xbuf[0:8, :] = jnp.zeros((8, EC), F4)

    @pl.when(r > 0)
    def _():
        xbuf[0:8, :] = xbuf[ROWS_STEP : ROWS_STEP + 8, :]

    xbuf[8:, :] = x[...].astype(F4)
    conv = bias[...] + taps[0:1, :] * xbuf[5 : 5 + ROWS_STEP, :]
    for i in range(1, KC):
        conv = conv + taps[i : i + 1, :] * xbuf[5 + i : 5 + i + ROWS_STEP, :]
    q = jax.nn.sigmoid(conv)
    u = conv * q
    u_out[...] = u
    slope_out[...] = q * (1.0 + conv * (1.0 - q))
    u_low = u.astype(BF)
    for s in range(PER_STEP):
        part = nt(u_low[own_runs(s)], xw[pf[O_KIND + r * PER_STEP + s]])
        part_out[pl.ds(pl.multiple_of(pf[O_POS + r * PER_STEP + s] * RUN, RUN), RUN), :] = part

    @pl.when(r == STEPS - 1)
    def _():
        near[...] = part_out[: LEN // 2, :]
        far[...] = part_out[LEN // 2 :, :]


def conv_call(pf, x_pre, taps, bias, w, first):
    return pl.pallas_call(
        conv_kernel,
        out_shape=[
            jax.ShapeDtypeStruct((LEN, EC), F4),
            pltpu.HBM((LEN, EC), F4),
            jax.ShapeDtypeStruct((LEN // 2, PROJ), F4),
            jax.ShapeDtypeStruct((LEN // 2, PROJ), F4),
            jax.ShapeDtypeStruct((MODES, PROJ, EC), BF),
            jax.ShapeDtypeStruct((MODES, R, EC), BF),
        ],
        grid_spec=pltpu.PrefetchScalarGridSpec(
            num_scalar_prefetch=1,
            grid=(STEPS,),
            in_specs=[
                step_spec(EC),
                whole((KC, EC)),
                whole((1, EC)),
                whole((PROJ, 256)),
                whole((R, 256)),
                pl.BlockSpec((16, TAIL_IN, EC), lambda i, pf: (0, first // TAIL_IN, 0)),
            ],
            out_specs=[
                step_spec(EC),
                step_spec(EC),
                whole((LEN // 2, PROJ)),
                whole((LEN // 2, PROJ)),
                whole((MODES, PROJ, EC)),
                whole((MODES, R, EC)),
            ],
            scratch_shapes=[
                pltpu.VMEM((ROWS_STEP + 8, EC), F4),
                pltpu.VMEM((LEN, PROJ), F4),
            ],
        ),
        compiler_params=params(14),
        cost_estimate=cost(1 << 28, 4 << 20, 1 << 20),
        name="conv_project",
    )(pf, x_pre, taps, bias, picker(PROJ, 10), picker(R, 8), in_hbm(w))


def softplus(v):
    e = jnp.exp(-jnp.abs(v))
    r = 1.0 / (1.0 + e)
    return jnp.maximum(v, 0.0) + jnp.log1p(e), jnp.where(v >= 0.0, r, e * r)


def halves(v):
    high = v.astype(BF)
    return high, (v - high.astype(F4)).astype(BF)


def masks():
    col = lax.broadcasted_iota(jnp.int32, (ROWS_STEP, SUB * NS), 1)
    row = lax.broadcasted_iota(jnp.int32, (ROWS_STEP, SUB * NS), 0)
    state = lax.broadcasted_iota(jnp.int32, (NS, SUB * NS), 0)
    state_col = lax.broadcasted_iota(jnp.int32, (NS, SUB * NS), 1)
    tiled = jnp.where(state_col % NS == state, 1.0, 0.0).astype(BF)
    return col // NS == row % SUB, tiled


def diagonals(values, own, tiled, out):
    for part, v in enumerate(halves(values)):
        out[part] = jnp.where(own, nn(v, tiled), 0.0).astype(BF).reshape(SUBS, SUB, SUB * NS)


def diagonal(diag, s):
    return jnp.concatenate([diag[0, s], diag[1, s]], axis=0)


def folded(values, own, tiled):
    high, low = halves(jnp.where(own, values, 0.0))
    return nt(high, tiled) + nt(low, tiled)


def columns_of(bct, bc):
    turned = jnp.concatenate([bc, jnp.zeros((ROWS_STEP, 128 - 2 * NS), F4)], axis=1).T
    for s in range(SUBS):
        bct[s] = turned[0 : 2 * NS, s * SUB : (s + 1) * SUB]


def scan_kernel(pf, u_in, z, *refs):
    ps, refs = refs[:PER_STEP], refs[PER_STEP:]
    (dtw, dtb, rates, skip, y, gated, d_out, slope_out, marks, *scratch) = refs
    state, dbuf, wbuf, hb0, hb1, bct, diag = scratch
    r = pl.program_id(0)

    @pl.when(r == 0)
    def _():
        state[...] = jnp.zeros_like(state)

    proj = joined(ps)
    low = proj[:, :R].astype(BF)
    v = jnp.concatenate(
        [nn(low[own_runs(s)], dtw[pf[O_KIND + r * PER_STEP + s]]) for s in range(PER_STEP)], axis=0
    )
    delta, slope = softplus(v + dtb[...])
    slope_out[...] = slope
    d_out[...] = delta
    u = u_in[...]
    dbuf[...] = delta
    wbuf[...] = delta * u
    y[...] = skip[...] * u
    rate = rates[...]
    columns_of(bct, proj[:, R:])
    diagonals(proj[:, R + NS :], *masks(), diag)

    def advance(s, h, hb):
        base = pl.multiple_of(s * SUB, SUB)
        marks[s] = h
        d_rows = dbuf[pl.ds(base, SUB), :]
        w_rows = wbuf[pl.ds(base, SUB), :]
        b_cols = bct[s]
        for i in range(SUB):
            a = jnp.exp2(d_rows[i : i + 1, :] * rate)
            h = a * h + b_cols[0:NS, i : i + 1] * w_rows[i : i + 1, :]
            hb[i * NS : (i + 1) * NS, :] = h.astype(BF)
        return h

    def sums(s, hb):
        both = nn(diagonal(diag, s), hb[...])
        y[pl.ds(pl.multiple_of(s * SUB, SUB), SUB), :] += both[0:SUB] + both[SUB:]

    def pair(k, h):
        sums(2 * k, hb0)
        h = advance(2 * k + 1, h, hb1)
        sums(2 * k + 1, hb1)
        return advance(2 * k + 2, h, hb0)

    h = advance(0, state[...], hb0)
    h = lax.fori_loop(0, SUBS // 2 - 1, pair, h)
    sums(SUBS - 2, hb0)
    state[...] = advance(SUBS - 1, h, hb1)
    sums(SUBS - 1, hb1)
    zf = z[...].astype(F4)
    gated[...] = (y[...] * (zf * jax.nn.sigmoid(zf))).astype(BF)


def scan_call(pf, u, z, proj, dtw, dtb, rates, skip):
    return pl.pallas_call(
        scan_kernel,
        out_shape=[
            pltpu.HBM((LEN, EC), F4),
            jax.ShapeDtypeStruct((LEN, EC), BF),
            pltpu.HBM((LEN, EC), F4),
            pltpu.HBM((LEN, EC), F4),
            pltpu.HBM((LEN // SUB, NS, EC), F4),
        ],
        grid_spec=pltpu.PrefetchScalarGridSpec(
            num_scalar_prefetch=1,
            grid=(STEPS,),
            in_specs=[step_spec(EC), step_spec(EC)]
            + pos_specs(PROJ)
            + [whole((MODES, R, EC)), whole((1, EC)), whole((NS, EC)), whole((1, EC))],
            out_specs=[
                step_spec(EC),
                step_spec(EC),
                step_spec(EC),
                step_spec(EC),
                pl.BlockSpec((SUBS, NS, EC), lambda i, pf: (i, 0, 0)),
            ],
            scratch_shapes=[
                pltpu.VMEM((NS, EC), F4),
                pltpu.VMEM((ROWS_STEP, EC), F4),
                pltpu.VMEM((ROWS_STEP, EC), F4),
                pltpu.VMEM((SUB * NS, EC), BF),
                pltpu.VMEM((SUB * NS, EC), BF),
                pltpu.VMEM((SUBS, 2 * NS, SUB), F4),
                pltpu.VMEM((2, SUBS, SUB, SUB * NS), BF),
            ],
        ),
        compiler_params=params(20),
        cost_estimate=cost(1 << 29, 12 << 20, 9 << 20),
        name="scan_forward",
    )(pf, u, z, *[proj] * PER_STEP, dtw, dtb, rates, skip)


def back_kernel(pf, u_in, d_in, slope, gg, z, y_in, *refs):
    ps, refs = refs[:PER_STEP], refs[PER_STEP:]
    (dtw, marks, rates, skip, usg, zgrad, near, far, dt_tail, alog, dtbg, skipg, *scratch) = refs
    (carry, dtwg, hprev, gb0, rb0, pb0, pc0, gb1, rb1, pb1, pc1, *scratch) = scratch
    wbuf, ybuf, pbuf, bct, diag, cbuf, bbuf, part = scratch
    r = pl.program_id(0)

    @pl.when(r == 0)
    def _():
        carry[...] = jnp.zeros_like(carry)
        dtwg[...] = jnp.zeros_like(dtwg)
        alog[...] = jnp.zeros_like(alog)
        dtbg[...] = jnp.zeros_like(dtbg)
        skipg[...] = jnp.zeros_like(skipg)

    delta = d_in[...]
    u = u_in[...]
    zf = z[...].astype(F4)
    q = jax.nn.sigmoid(zf)
    gf = gg[...].astype(F4)
    yg = gf * (zf * q)
    zgrad[...] = (gf * y_in[...] * (q * (1.0 + zf * (1.0 - q)))).astype(BF)
    wbuf[...] = delta * u
    ybuf[...] = yg
    skipg[...] += jnp.sum(yg * u, axis=0, keepdims=True)
    rate = rates[...]
    proj = joined(ps)
    columns_of(bct, proj[:, R:])
    own, tiled = masks()
    diagonals(proj[:, R : R + NS], own, tiled, diag)

    ones = jnp.where(own[:SUB], 1.0, 0.0).astype(BF)

    def lanes(v):
        return (v[:, 0:128] + v[:, 128:256]) + (v[:, 256:384] + v[:, 384:512])

    def retreat(s, carried, bufs):
        gb, rb, pb, pc = bufs
        ag, al = carried
        base = pl.multiple_of(s * SUB, SUB)
        d_rows = d_in[pl.ds(base, SUB), :]
        w_rows = wbuf[pl.ds(base, SUB), :]
        y_rows = ybuf[pl.ds(base, SUB), :]
        bc_cols = bct[s]
        h = marks[s]
        for i in range(SUB):
            hprev[i] = h
            a = jnp.exp2(d_rows[i : i + 1, :] * rate)
            h = a * h + bc_cols[0:NS, i : i + 1] * w_rows[i : i + 1, :]
            pc[i * NS : (i + 1) * NS, :] = lanes(h * y_rows[i : i + 1, :]).astype(BF)
        for i in reversed(range(SUB)):
            g = ag + bc_cols[NS:, i : i + 1] * y_rows[i : i + 1, :]
            gb[i * NS : (i + 1) * NS, :] = g.astype(BF)
            pb[i * NS : (i + 1) * NS, :] = lanes(g * w_rows[i : i + 1, :]).astype(BF)
            ag = jnp.exp2(d_rows[i : i + 1, :] * rate) * g
            rp = rate * (ag * hprev[i])
            rb[i * NS : (i + 1) * NS, :] = rp.astype(BF)
            al = al + d_rows[i : i + 1, :] * rp
        return ag, al

    full = jnp.ones((SUB, 128), BF)

    def sums(s, bufs):
        gb, rb, pb, pc = bufs
        at = pl.ds(pl.multiple_of(s * SUB, SUB), SUB)
        both = nn(diagonal(diag, s), gb[...])
        bsum = both[0:SUB] + both[SUB:]
        dsum = nn(ones, rb[...])
        cbuf[at, :] = nt(full, pc[...])
        bbuf[at, :] = nt(full, pb[...])
        usg[at, :] = d_in[at, :] * bsum + skip[...] * ybuf[at, :]
        pbuf[at, :] = dsum * LN2 + u_in[at, :] * bsum

    even, odd = (gb0, rb0, pb0, pc0), (gb1, rb1, pb1, pc1)

    def pair(k, carried):
        s = SUBS - 1 - 2 * k
        sums(s, even)
        carried = retreat(s - 1, carried, odd)
        sums(s - 1, odd)
        return retreat(s - 2, carried, even)

    carried = retreat(SUBS - 1, (carry[...], jnp.zeros((NS, EC), F4)), even)
    carried = lax.fori_loop(0, SUBS // 2 - 1, pair, carried)
    sums(1, even)
    ag, al = retreat(0, carried, odd)
    sums(0, odd)
    carry[...] = ag
    alog[...] += al * LN2
    pre = pbuf[...] * slope[...]
    dtbg[...] += jnp.sum(pre, axis=0, keepdims=True)
    pre_low = pre.astype(BF)
    bgrad = folded(bbuf[...], own, tiled)
    cgrad = folded(cbuf[...], own, tiled)
    low = proj[:, :R].astype(BF)
    for s in range(PER_STEP):
        run = (STEPS - 1 - r) * PER_STEP + s
        kind = pf[O_KIND + run]
        at = pl.ds(pl.multiple_of(pf[O_POS + run] * RUN, RUN), RUN)
        part[at, :R] = nt(pre_low[own_runs(s)], dtw[kind])
        part[at, R : R + NS] = bgrad[own_runs(s)]
        part[at, R + NS :] = cgrad[own_runs(s)]
        dtwg[kind] += tn(low[own_runs(s)], pre_low[own_runs(s)])

    @pl.when(r == STEPS - 1)
    def _():
        near[...] = part[: LEN // 2, :]
        far[...] = part[LEN // 2 :, :]
        for s in range(16):
            for m in range(MODES):
                dt_tail[s, m * 8 : (m + 1) * 8, :] = dtwg[m, s * 8 : (s + 1) * 8, :]


def back_call(pf, u, delta, slope, gg, z, y, proj, dtw, marks, rates, skip):
    return pl.pallas_call(
        back_kernel,
        out_shape=[
            jax.ShapeDtypeStruct((LEN, EC), F4),
            jax.ShapeDtypeStruct((LEN, EC), BF),
            jax.ShapeDtypeStruct((LEN // 2, PROJ), F4),
            jax.ShapeDtypeStruct((LEN // 2, PROJ), F4),
            jax.ShapeDtypeStruct((16, MODES * 8, EC), F4),
            jax.ShapeDtypeStruct((NS, EC), F4),
            jax.ShapeDtypeStruct((1, EC), F4),
            jax.ShapeDtypeStruct((1, EC), F4),
        ],
        grid_spec=pltpu.PrefetchScalarGridSpec(
            num_scalar_prefetch=1,
            grid=(STEPS,),
            in_specs=[step_spec(EC, True)] * 6
            + pos_specs(PROJ, True)
            + [
                whole((MODES, R, EC)),
                pl.BlockSpec((SUBS, NS, EC), lambda i, pf: (STEPS - 1 - i, 0, 0)),
                whole((NS, EC)),
                whole((1, EC)),
            ],
            out_specs=[
                step_spec(EC, True),
                step_spec(EC, True),
                whole((LEN // 2, PROJ)),
                whole((LEN // 2, PROJ)),
                whole((16, MODES * 8, EC)),
                whole((NS, EC)),
                whole((1, EC)),
                whole((1, EC)),
            ],
            scratch_shapes=[
                pltpu.VMEM((NS, EC), F4),
                pltpu.VMEM((MODES, R, EC), F4),
                pltpu.VMEM((SUB, NS, EC), F4),
                *([pltpu.VMEM((SUB * NS, EC), BF)] * 2 + [pltpu.VMEM((SUB * NS, 128), BF)] * 2) * 2,
                pltpu.VMEM((ROWS_STEP, EC), F4),
                pltpu.VMEM((ROWS_STEP, EC), F4),
                pltpu.VMEM((ROWS_STEP, EC), F4),
                pltpu.VMEM((SUBS, 2 * NS, SUB), F4),
                pltpu.VMEM((2, SUBS, SUB, SUB * NS), BF),
                pltpu.VMEM((ROWS_STEP, SUB * NS), F4),
                pltpu.VMEM((ROWS_STEP, SUB * NS), F4),
                pltpu.VMEM((LEN, PROJ), F4),
            ],
        ),
        compiler_params=params(24),
        cost_estimate=cost(1 << 30, 14 << 20, 9 << 20),
        name="scan_backward",
    )(pf, u, delta, slope, gg, z, y, *[proj] * PER_STEP, dtw, marks, rates, skip)


def conv_back_kernel(pf, *refs):
    pgs, refs = refs[:PER_STEP], refs[PER_STEP:]
    (xw, usg, u, slope, x_now, x_before, taps, out, x_tail, cwg, cbg, gbuf, xbuf, xwg) = refs
    r = pl.program_id(0)

    @pl.when(r == 0)
    def _():
        xwg[...] = jnp.zeros_like(xwg)
        cwg[...] = jnp.zeros_like(cwg)
        cbg[...] = jnp.zeros_like(cbg)
        gbuf[ROWS_STEP:, :] = jnp.zeros((8, EC), F4)

    @pl.when(r > 0)
    def _():
        gbuf[ROWS_STEP:, :] = gbuf[0:8, :]

    u_low = u[...].astype(BF)
    kinds = [pf[O_KIND + (STEPS - 1 - r) * PER_STEP + s] for s in range(PER_STEP)]
    u_grad = usg[...] + jnp.concatenate([nn(pgs[s][...], xw[kinds[s]]) for s in range(PER_STEP)], axis=0)
    grad = u_grad * slope[...]
    gbuf[0:ROWS_STEP, :] = grad
    cbg[...] += jnp.sum(grad, axis=0, keepdims=True)
    before = x_before[...].astype(F4)[16 - 8 :, :]
    xbuf[0:8, :] = jnp.where(r == STEPS - 1, jnp.zeros_like(before), before)
    xbuf[8:, :] = x_now[...].astype(F4)
    back = taps[KC - 1 : KC, :] * grad
    for i in range(KC):
        cwg[i : i + 1, :] += jnp.sum(grad * xbuf[5 + i : 5 + i + ROWS_STEP, :], axis=0, keepdims=True)
        if i < KC - 1:
            back = back + taps[i : i + 1, :] * gbuf[KC - 1 - i : KC - 1 - i + ROWS_STEP, :]
    out[...] = back.astype(BF)
    for s in range(PER_STEP):
        xwg[kinds[s]] += tn(pgs[s][...], u_low[own_runs(s)])

    @pl.when(r == STEPS - 1)
    def _():
        for s in range(16):
            for m in range(MODES):
                x_tail[s, m * 10 : (m + 1) * 10, :] = xwg[m, s * 10 : (s + 1) * 10, :]
            x_tail[s, MODES * 10 :, :] = jnp.zeros((TAIL_OUT - 24 - MODES * 10, EC), F4)


def conv_back_call(pf, pg, xw, usg, u, slope, x_pre, taps):
    before = ROWS_STEP // 16
    return pl.pallas_call(
        conv_back_kernel,
        out_shape=[
            jax.ShapeDtypeStruct((LEN, EC), BF),
            jax.ShapeDtypeStruct((16, TAIL_OUT - 24, EC), F4),
            jax.ShapeDtypeStruct((KC, EC), F4),
            jax.ShapeDtypeStruct((1, EC), F4),
        ],
        grid_spec=pltpu.PrefetchScalarGridSpec(
            num_scalar_prefetch=1,
            grid=(STEPS,),
            in_specs=pos_specs(PROJ, True)
            + [
                whole((MODES, PROJ, EC)),
                step_spec(EC, True),
                step_spec(EC, True),
                step_spec(EC, True),
                step_spec(EC, True),
                pl.BlockSpec(
                    (16, EC), lambda i, pf: (jnp.maximum((STEPS - 1 - i) * before - 1, 0), 0)
                ),
                whole((KC, EC)),
            ],
            out_specs=[
                step_spec(EC, True),
                whole((16, TAIL_OUT - 24, EC)),
                whole((KC, EC)),
                whole((1, EC)),
            ],
            scratch_shapes=[
                pltpu.VMEM((ROWS_STEP + 8, EC), F4),
                pltpu.VMEM((ROWS_STEP + 8, EC), F4),
                pltpu.VMEM((MODES, PROJ, EC), F4),
            ],
        ),
        compiler_params=params(16),
        cost_estimate=cost(1 << 29, 8 << 20, 1 << 20),
        name="conv_backward",
    )(pf, *[pg] * PER_STEP, xw, usg, u, slope, x_pre, x_pre, taps)


def ring(v, axis, step):
    return lax.ppermute(v, axis, [(i, (i + step) % 4) for i in range(4)])


def across(v):
    return lax.ppermute(v, "c", [(0, 1), (1, 0)])


def after(value, *others):
    return lax.optimization_barrier((value, others))[0]


def add(*values):
    total = values[0].astype(F4)
    for value in values[1:]:
        total = total + value.astype(F4)
    return total


def spread_chan(rows):
    left = ring(rows, "y", 1)
    right = ring(rows, "y", -1)
    far = [ring(left[:RUN], "y", 1), ring(right[RUN:], "y", -1)]
    near = jnp.concatenate([rows, right, *far, left], axis=0)
    return jnp.concatenate([near, across(near)], axis=0)


def collect_chan(near, far):
    pair = add(near, across(far)).astype(BF).reshape(4, 2 * RUN, D)
    own, right, far_first, far_second, left = pair[0], pair[1], pair[2, :RUN], pair[2, RUN:], pair[3]
    came = ring(far_first, "y", 1)
    came_back = ring(far_second, "y", -1)
    right = jnp.concatenate([add(right[:RUN], came).astype(BF), right[RUN:]], axis=0)
    left = jnp.concatenate([left[:RUN], add(left[RUN:], came_back).astype(BF)], axis=0)
    return add(own, ring(right, "y", 1), ring(left, "y", -1))


def direct(v, axis):
    return [v, ring(v, axis, -1), ring(v, axis, 2), ring(v, axis, 1)]


def sum_chan(near, far, finish, fill=None):
    pair = add(near, across(far)).reshape(4, LEN // 8, near.shape[1])
    came = [ring(pair[1], "y", 1), ring(pair[2], "y", 2), ring(pair[3], "y", -1)]
    filled = None
    if fill:
        filled = fill(pair)
        came = after(came, filled)
    mine = jnp.concatenate(direct(finish(add(pair[0], *came)), "y"), axis=0)
    return jnp.concatenate([mine, across(mine)], axis=0), filled


def sum_axis(v, axis):
    v = jnp.roll(v, -lax.axis_index(axis), 0)
    return add(v[0], ring(v[1], axis, 1), ring(v[2], axis, 2), ring(v[3], axis, -1))


def sum_pair(v):
    place = lax.axis_index("c")
    keep = lax.dynamic_index_in_dim(v, place, 2, False)
    give = lax.dynamic_index_in_dim(v, 1 - place, 2, False)
    return sum_axis(jnp.swapaxes(keep + across(give), 0, 1), "y")


def sum_seq(v):
    return sum_axis(sum_axis(v.reshape(4, 4, v.shape[1]), "z"), "x")


def local(
    layer_input, kinds, norm_gain, in_weight, conv_weight, conv_bias, x_weight, dt_weight,
    dt_bias, a_log, d_skip, out_weight, cotangent,
):
    place_y, place_c = lax.axis_index("y"), lax.axis_index("c")
    chan = place_y * 2 + place_c
    gain = norm_gain.astype(F4)
    taps = conv_weight.astype(F4)
    cbias = conv_bias.astype(F4)[None, :]
    dtb = dt_bias.astype(F4)[None, :]
    a_own = lax.dynamic_slice_in_dim(a_log, chan * EC, EC, 1).astype(F4)
    rates = -jnp.exp(a_own) * LOG2E
    skip = lax.dynamic_slice_in_dim(d_skip, chan * EC, EC, 0).astype(F4)[None, :]

    x32 = layer_input.astype(F4)
    rms = lax.rsqrt(jnp.mean(x32 * x32, axis=1, keepdims=True) + 1e-05)
    normed = (x32 * rms * gain[None, :]).astype(BF)

    early_w = lax.all_gather(
        jnp.concatenate(
            [
                in_weight[:, :, 0, :].reshape(ROWS, EC),
                in_weight[:, :, 1, :].reshape(ROWS, EC),
                jnp.pad(x_weight, ((0, 0), (0, 6), (0, 0))).reshape(48, EC),
                jnp.pad(dt_weight, ((0, 0), (0, 8), (0, 0))).reshape(48, EC),
            ],
            axis=0,
        ),
        SEQ,
    )
    pf = slot_plan(kinds)
    xs = spread_chan(normed)
    cs = spread_chan(cotangent)
    out_w = lax.all_gather(after(out_weight.reshape(ROWS, EC), xs, cs), SEQ)
    rates, skip, taps, cbias, dtb, xs = after((rates, skip, taps, cbias, dtb, xs), pf)
    early_w = after(early_w, rates, skip, taps, cbias, dtb, xs)
    x_pre = down(pf, in_hbm(xs), early_w, "project_scan")
    u, conv_slope, near, far, xw, dtw = conv_call(pf, x_pre, taps, cbias, early_w, 2 * ROWS)
    proj, z = sum_chan(
        near,
        far,
        lambda total: total,
        lambda pair: down(pf, after(xs, pair), early_w, "project_gate", MODES),
    )
    y, gated, delta, slope, marks = scan_call(pf, u, z, proj, dtw, dtb, rates, skip)

    out_part = outer(pf, "out_weight_grad", cs, gated, ROWS)
    out_sum = lax.psum_scatter(out_part, SEQ, scatter_dimension=0).astype(F4)
    gg = down(pf, in_hbm(after(cs, out_part)), out_w, "project_cotangent")
    usg, zgrad, near, far, dt_tail, alog, dtbg, skipg = back_call(
        pf, u, delta, slope, gg, z, y, proj, dtw, marks, rates, skip
    )
    pg, weights_part = sum_chan(
        near,
        far,
        lambda total: total.astype(BF),
        lambda pair: outer(pf, "gate_weight_grad", xs, after(zgrad, pair), 2 * ROWS + TAIL_OUT),
    )
    xgrad, x_tail, cwg, cbg = conv_back_call(pf, pg, xw, usg, u, conv_slope, x_pre, taps)
    weights_part = outer(
        pf,
        "scan_weight_grad",
        xs,
        after(xgrad, out_sum),
        2 * ROWS + TAIL_OUT,
        ROWS,
        weights_part,
        (dt_tail, x_tail),
    )
    weights_sum = lax.psum_scatter(weights_part, SEQ, scatter_dimension=0).astype(F4)

    zgrad, gated = after((zgrad, gated), weights_part)
    branch = collect_chan(*up(pf, "project_out", (gated, out_w, 0)))
    mixed = (x32 + branch).astype(BF)
    near, far, gain_part = up(
        pf, "input_grad", (xgrad, early_w, 0), (zgrad, early_w, MODES), xs=xs
    )
    ngrad = collect_chan(near, far) * gain[None, :]
    x_grad = (
        cotangent.astype(F4)
        + rms * ngrad
        - x32 * (rms * rms * rms) * jnp.mean(ngrad * x32, axis=1, keepdims=True)
    )
    in_grad = jnp.stack(
        [
            weights_sum[ROWS : 2 * ROWS].reshape(MODES, 128, EC),
            weights_sum[:ROWS].reshape(MODES, 128, EC),
        ],
        axis=2,
    )
    out_grad = out_sum.reshape(MODES, 128, EC)
    dt_w_grad = weights_sum[2 * ROWS : 2 * ROWS + 24].reshape(MODES, 8, EC)
    x_w_grad = weights_sum[2 * ROWS + 24 : 2 * ROWS + 54].reshape(MODES, 10, EC)
    gain_part = sum_pair((gain_part[0] / gain).reshape(16, 4, 2, 16))
    small = jnp.concatenate([cwg, cbg, dtbg, skipg, alog], axis=0)
    small = jnp.swapaxes(small.reshape(23, 16, 32), 0, 1).reshape(16, 23 * 32)
    small = sum_seq(jnp.concatenate([small, gain_part, jnp.zeros((16, 16), F4)], axis=1))
    gain_grad = small[23 * 32 : 24 * 32 - 16]
    moves = [(s * 8 + c, c * 16 + s) for s in range(16) for c in range(8)]
    own = lax.ppermute(small[: 23 * 32].reshape(23, 32), ("z", "x", "y", "c"), moves)
    return (
        mixed,
        x_grad,
        gain_grad,
        in_grad,
        own[0:4],
        own[4],
        x_w_grad,
        dt_w_grad,
        own[5],
        own[7:],
        own[6],
        out_grad,
    )


def solution(mesh):
    fine = Mesh(mesh.devices.reshape(4, 4, 4, 2), ("z", "x", "y", "c"))
    rows = ("z", "x", "y", "c")
    return jax.shard_map(
        local,
        mesh=fine,
        in_specs=(
            P(rows, None),
            P(SEQ),
            P(),
            P(None, SEQ, None, CHAN),
            P(None, CHAN),
            P(CHAN),
            P(None, SEQ, CHAN),
            P(None, SEQ, CHAN),
            P(CHAN),
            P(),
            P(),
            P(None, SEQ, CHAN),
            P(rows, None),
        ),
        out_specs=(
            P(rows, None),
            P(rows, None),
            P(rows),
            P(None, SEQ, None, CHAN),
            P(None, rows),
            P(rows),
            P(None, SEQ, CHAN),
            P(None, SEQ, CHAN),
            P(rows),
            P(None, rows),
            P(rows),
            P(None, SEQ, CHAN),
        ),
        check_vma=False,
    )
```

```python
import functools

import jax
import jax.numpy as jnp
import numpy as np
from jax import lax
from jax.experimental import pallas as pl
from jax.experimental.pallas import tpu as pltpu
from jax.sharding import Mesh
from jax.sharding import PartitionSpec as P

NS = 16
KC = 4
R = 128
MODES = 3
RUN = 64
RUNS = 16
LEN = 1024
D = 2048
EC = 512
PER = 4
BLK = RUN * PER
NBLK = 6
SLOTS = NBLK * PER
SUB = 16
NSUB = RUN // SUB
LOG2E = 1.4426950408889634
LN2 = 0.6931471805599453
ROWS = MODES * 128
TAIL_IN = 64
TAIL_OUT = 64
PROJ = R + 2 * NS

BF = jnp.bfloat16
F4 = jnp.float32

O_RUN = 0
O_VALID = SLOTS
O_PLACE = 2 * SLOTS
O_BK = 3 * SLOTS
O_TOTAL = O_BK + NBLK
O_KIND = O_TOTAL + 1
O_POS = O_KIND + RUNS
O_FIRST = O_POS + RUNS
O_COUNT = O_FIRST + MODES

SEQ = ("z", "x")
CHAN = ("y", "c")


def params(limit=56):
    return pltpu.CompilerParams(vmem_limit_bytes=limit << 20)


def in_hbm(x):
    return pltpu.with_memory_space_constraint(x, pltpu.HBM)


def cost(flops, moved, trans=0):
    return pl.CostEstimate(flops=int(flops), bytes_accessed=int(moved), transcendentals=int(trans))


def nt(a, b):
    return lax.dot_general(a, b, (((1,), (1,)), ((), ())), preferred_element_type=F4)


def tn(a, b):
    return lax.dot_general(a, b, (((0,), (0,)), ((), ())), preferred_element_type=F4)


def nn(a, b):
    return jnp.dot(a, b, preferred_element_type=F4)


def whole(shape):
    zeros = (0,) * len(shape)
    return pl.BlockSpec(shape, lambda i, pf: zeros)


def slot_plan(kinds):
    me_y, me_c = lax.axis_index("y"), lax.axis_index("c")
    run_kind = kinds.reshape(RUNS, RUN)[:, 0]
    one_hot = (run_kind[:, None] == jnp.arange(MODES, dtype=jnp.int32)[None, :]).astype(jnp.int32)
    count = jnp.sum(one_hot, axis=0)
    blocks = (count + PER - 1) // PER
    first = jnp.cumsum(blocks) - blocks
    rank = jnp.cumsum(one_hot, axis=0) - one_hot
    slot = jnp.sum(one_hot * (PER * first[None, :] + rank), axis=1)
    slots = jnp.arange(SLOTS, dtype=jnp.int32)
    hit = (slot[None, :] == slots[:, None]).astype(jnp.int32)
    valid = jnp.sum(hit, axis=1)
    head = (slot[None, :] == (slots // PER * PER)[:, None]).astype(jnp.int32)
    runs = jnp.arange(RUNS, dtype=jnp.int32)
    run_of = jnp.sum(jnp.where(valid[:, None] > 0, hit, head) * runs[None, :], axis=1)
    total = jnp.sum(blocks)
    place = jnp.minimum(jnp.arange(NBLK, dtype=jnp.int32), total - 1)
    block_kind = jnp.sum((place[:, None] >= first[None, 1:]).astype(jnp.int32), axis=1)

    def position(run):
        core = jnp.where((run // 2) % 2 == me_c, 0, 1)
        return core * 8 + ((run // 4 - me_y) % 4) * 2 + run % 2

    return jnp.concatenate(
        [
            run_of,
            valid,
            position(run_of),
            block_kind,
            total[None],
            run_kind,
            position(runs),
            first,
            blocks,
        ]
    ).astype(jnp.int32)


def slot_run(pf, b, s):
    return pl.multiple_of(pf[O_RUN + b * PER + s] * RUN, RUN)


def slot_place(pf, b, s):
    return pl.multiple_of(pf[O_PLACE + b * PER + s] * RUN, RUN)


def live(i, pf):
    return jnp.minimum(i, pf[O_TOTAL] - 1)


def seq_spec(first):
    return pl.BlockSpec((16, 128, EC), lambda i, pf: (0, first + pf[O_BK + i], 0))


def row_specs():
    def one(s):
        return pl.BlockSpec((RUN, D), lambda i, pf: (pf[O_PLACE + live(i, pf) * PER + s], 0))

    return [one(s) for s in range(PER)]


def down_kernel(pf, x0, x1, x2, x3, w, out):
    b = pl.program_id(0)

    @pl.when(b < pf[O_TOTAL])
    def _():
        rows = jnp.concatenate([x0[...], x1[...], x2[...], x3[...]], axis=0)
        value = nn(rows, w[...].reshape(D, EC)).astype(BF)
        for s in range(PER):
            out[pl.ds(slot_run(pf, b, s), RUN), :] = value[s * RUN : (s + 1) * RUN]


def down(pf, x, w, name, first=0):
    return pl.pallas_call(
        down_kernel,
        out_shape=jax.ShapeDtypeStruct((LEN, EC), BF),
        grid_spec=pltpu.PrefetchScalarGridSpec(
            num_scalar_prefetch=1,
            grid=(NBLK,),
            in_specs=row_specs() + [seq_spec(first)],
            out_specs=whole((LEN, EC)),
        ),
        compiler_params=params(16),
        cost_estimate=cost(6 * 2 * BLK * D * EC, 14 << 20),
        name=name,
    )(pf, x, x, x, x, in_hbm(w))


def up_kernel(pf, *refs, pairs, with_gain):
    if with_gain:
        xs = refs[2 * pairs : 2 * pairs + PER]
        near, far, gain, both = refs[2 * pairs + PER :]
    else:
        near, far, both = refs[2 * pairs :]
    b = pl.program_id(0)

    if with_gain:

        @pl.when(b == 0)
        def _():
            gain[...] = jnp.zeros_like(gain)

    @pl.when(b < pf[O_TOTAL])
    def _():
        tile = None
        for p in range(pairs):
            g, w = refs[2 * p], refs[2 * p + 1]
            rows = jnp.concatenate([g[pl.ds(slot_run(pf, b, s), RUN), :] for s in range(PER)], axis=0)
            term = nt(rows, w[...].reshape(D, EC))
            tile = term if p == 0 else tile + term
        for s in range(PER):
            part = tile[s * RUN : (s + 1) * RUN]
            both[pl.ds(slot_place(pf, b, s), RUN), :] = part.astype(BF)
            if with_gain:
                term = jnp.sum(part * xs[s][...].astype(F4), axis=0, keepdims=True)
                gain[...] += jnp.where(pf[O_VALID + b * PER + s] > 0, term, jnp.zeros_like(term))

    @pl.when(b == NBLK - 1)
    def _():
        near[...] = both[: LEN // 2, :]
        far[...] = both[LEN // 2 :, :]


def up(pf, name, *terms, xs=None):
    side = whole((LEN // 2, D))
    args, specs = [], []
    for g, w, first in terms:
        args += [g, in_hbm(w)]
        specs += [whole((LEN, EC)), seq_spec(first)]
    out_shape, out_specs = [pltpu.HBM((LEN // 2, D), BF)] * 2, [side] * 2
    if xs is not None:
        args += [in_hbm(xs)] * PER
        specs += row_specs()
        out_shape = out_shape + [jax.ShapeDtypeStruct((1, D), F4)]
        out_specs = out_specs + [whole((1, D))]
    return pl.pallas_call(
        functools.partial(up_kernel, pairs=len(terms), with_gain=xs is not None),
        out_shape=out_shape,
        grid_spec=pltpu.PrefetchScalarGridSpec(
            num_scalar_prefetch=1,
            grid=(NBLK,),
            in_specs=specs,
            out_specs=out_specs,
            scratch_shapes=[pltpu.VMEM((LEN, D), BF)],
        ),
        compiler_params=params(32),
        cost_estimate=cost(len(terms) * 6 * 2 * BLK * D * EC, 14 << 20),
        name=name,
    )(pf, *args)


def outer_kernel(pf, x_in, g_in, *refs, tail):
    out, sorted_g = refs[-2:]

    @pl.when(pl.program_id(0) == 0)
    def _():
        for b in range(NBLK):
            for s in range(PER):
                rows = g_in[pl.ds(slot_run(pf, b, s), RUN), :]
                rows = jnp.where(pf[O_VALID + b * PER + s] > 0, rows, jnp.zeros_like(rows))
                at = b * BLK + s * RUN
                sorted_g[at : at + RUN, :] = rows

    def one_kind(m, carry):
        first, count = pf[O_FIRST + m], pf[O_COUNT + m]
        rows = pl.ds(pl.multiple_of(m * 128, 128), 128)

        @pl.when(count == 0)
        def _():
            for s in range(4):
                out[s, rows, :] = jnp.zeros((128, EC), BF)

        for n in range(1, RUNS // PER + 1):

            @pl.when(count == n)
            def _():
                x = jnp.concatenate(
                    [x_in[pl.ds(slot_place(pf, first, s), RUN), :] for s in range(n * PER)], axis=0
                )
                g = sorted_g[pl.ds(pl.multiple_of(first * BLK, BLK), n * BLK), :]
                value = tn(x, g).astype(BF)
                for s in range(4):
                    out[s, rows, :] = value[s * 128 : (s + 1) * 128, :]

        return carry

    lax.fori_loop(0, MODES, one_kind, 0)
    if tail:
        dt_tail, x_tail = refs[:2]
        for s in range(4):
            out[s, ROWS:, :] = jnp.concatenate([dt_tail[s], x_tail[s]], axis=0).astype(BF)


def outer(pf, name, x, g, held_rows, first=0, held=None, tails=()):
    rows = ROWS + (TAIL_OUT if tails else 0)
    specs = [pl.BlockSpec((LEN, 512), lambda i, pf: (0, i)), whole((LEN, EC))]
    args = [x, g]
    if tails:
        specs += [
            pl.BlockSpec((4, 24, EC), lambda i, pf: (i, 0, 0)),
            pl.BlockSpec((4, TAIL_OUT - 24, EC), lambda i, pf: (i, 0, 0)),
        ]
        args += tails
    aliases = {}
    if held is not None:
        specs.append(pl.BlockSpec(memory_space=pl.ANY))
        args.append(held)
        aliases = {len(args): 0}
    if first % rows == 0:
        out_spec = pl.BlockSpec((4, rows, EC), lambda i, pf: (i, first // rows, 0))
    else:
        out_spec = pl.BlockSpec((pl.Element(4), pl.Element(rows), pl.Element(EC)), lambda i, pf: (4 * i, first, 0))
    return pl.pallas_call(
        functools.partial(outer_kernel, tail=bool(tails)),
        out_shape=pltpu.HBM((16, held_rows, EC), BF),
        grid_spec=pltpu.PrefetchScalarGridSpec(
            num_scalar_prefetch=1,
            grid=(4,),
            in_specs=specs,
            out_specs=out_spec,
            scratch_shapes=[pltpu.VMEM((NBLK * BLK, EC), BF)],
        ),
        input_output_aliases=aliases,
        compiler_params=params(20),
        cost_estimate=cost(6 * 2 * BLK * D * EC, 14 << 20),
        name=name,
    )(pf, *args)


def unpack_kernel(sums, in_grad, x_w_grad, dt_w_grad):
    for m in range(MODES):
        in_grad[m, :, 0, :] = sums[ROWS + m * 128 : ROWS + (m + 1) * 128, :].astype(F4)
        in_grad[m, :, 1, :] = sums[m * 128 : (m + 1) * 128, :].astype(F4)
        tail = sums[2 * ROWS :, :].astype(F4)
        dt_w_grad[m] = tail[m * 8 : (m + 1) * 8]
        x_w_grad[m] = tail[24 + m * 10 : 24 + (m + 1) * 10]


def unpack(sums):
    return pl.pallas_call(
        unpack_kernel,
        out_shape=[
            jax.ShapeDtypeStruct((MODES, 128, 2, EC), F4),
            jax.ShapeDtypeStruct((MODES, 10, EC), F4),
            jax.ShapeDtypeStruct((MODES, 8, EC), F4),
        ],
        compiler_params=params(12),
        cost_estimate=cost(0, 3 << 20),
        name="unpack_sums",
    )(in_hbm(sums))


def pickers():
    col = np.arange(256)[None, :]
    i = np.arange(PROJ)[:, None]
    k = np.arange(R)[:, None]
    slot, row = k // 8 * 16, k % 8
    dt = [(row < 6) & (col == slot + 10 + row)]
    dt += [(row >= 6) & (col == slot + m * 2 + row - 6) for m in range(MODES)]
    return jnp.asarray(col == i // 10 * 16 + i % 10, BF), jnp.asarray(np.stack(dt), BF)


STEPS = 4
PER_STEP = RUNS // STEPS
ROWS_STEP = LEN // STEPS
SUBS = ROWS_STEP // SUB


def step_spec(width, back=False):
    if back:
        return pl.BlockSpec((ROWS_STEP, width), lambda i, pf: (STEPS - 1 - i, 0))
    return pl.BlockSpec((ROWS_STEP, width), lambda i, pf: (i, 0))


def pos_specs(width, back=False):
    def one(s):
        if back:
            return pl.BlockSpec((RUN, width), lambda i, pf: (pf[O_POS + (STEPS - 1 - i) * PER_STEP + s], 0))
        return pl.BlockSpec((RUN, width), lambda i, pf: (pf[O_POS + i * PER_STEP + s], 0))

    return [one(s) for s in range(PER_STEP)]


def joined(refs):
    return jnp.concatenate([ref[...] for ref in refs], axis=0)


def own_runs(s):
    return slice(s * RUN, (s + 1) * RUN)


def conv_kernel(pf, x, taps, bias, pick_x, pick_dt, w, u_out, slope_out, near, far, xw, dtw, xbuf, part_out):
    r = pl.program_id(0)

    @pl.when(r == 0)
    def _():
        last = w[:, 48:, :].reshape(256, EC)
        for m in range(MODES):
            rows = w[:, m * 16 : (m + 1) * 16, :].reshape(256, EC)
            xw[m] = nn(pick_x[...], rows).astype(BF)
            dtw[m] = (nn(pick_dt[0], rows) + nn(pick_dt[1 + m], last)).astype(BF)
        xbuf[0:8, :] = jnp.zeros((8, EC), F4)

    @pl.when(r > 0)
    def _():
        xbuf[0:8, :] = xbuf[ROWS_STEP : ROWS_STEP + 8, :]

    xbuf[8:, :] = x[...].astype(F4)
    conv = bias[...] + taps[0:1, :] * xbuf[5 : 5 + ROWS_STEP, :]
    for i in range(1, KC):
        conv = conv + taps[i : i + 1, :] * xbuf[5 + i : 5 + i + ROWS_STEP, :]
    q = jax.nn.sigmoid(conv)
    u = conv * q
    u_out[...] = u
    slope_out[...] = q * (1.0 + conv * (1.0 - q))
    u_low = u.astype(BF)
    for s in range(PER_STEP):
        part = nt(u_low[own_runs(s)], xw[pf[O_KIND + r * PER_STEP + s]])
        part_out[pl.ds(pl.multiple_of(pf[O_POS + r * PER_STEP + s] * RUN, RUN), RUN), :] = part

    @pl.when(r == STEPS - 1)
    def _():
        near[...] = part_out[: LEN // 2, :]
        far[...] = part_out[LEN // 2 :, :]


def conv_call(pf, x_pre, taps, bias, w, first):
    return pl.pallas_call(
        conv_kernel,
        out_shape=[
            jax.ShapeDtypeStruct((LEN, EC), F4),
            pltpu.HBM((LEN, EC), F4),
            jax.ShapeDtypeStruct((LEN // 2, PROJ), F4),
            jax.ShapeDtypeStruct((LEN // 2, PROJ), F4),
            jax.ShapeDtypeStruct((MODES, PROJ, EC), BF),
            jax.ShapeDtypeStruct((MODES, R, EC), BF),
        ],
        grid_spec=pltpu.PrefetchScalarGridSpec(
            num_scalar_prefetch=1,
            grid=(STEPS,),
            in_specs=[
                step_spec(EC),
                whole((KC, EC)),
                whole((1, EC)),
                whole((PROJ, 256)),
                whole((1 + MODES, R, 256)),
                pl.BlockSpec((16, TAIL_IN, EC), lambda i, pf: (0, first // TAIL_IN, 0)),
            ],
            out_specs=[
                step_spec(EC),
                step_spec(EC),
                whole((LEN // 2, PROJ)),
                whole((LEN // 2, PROJ)),
                whole((MODES, PROJ, EC)),
                whole((MODES, R, EC)),
            ],
            scratch_shapes=[
                pltpu.VMEM((ROWS_STEP + 8, EC), F4),
                pltpu.VMEM((LEN, PROJ), F4),
            ],
        ),
        compiler_params=params(14),
        cost_estimate=cost(1 << 28, 4 << 20, 1 << 20),
        name="conv_project",
    )(pf, x_pre, taps, bias, *pickers(), in_hbm(w))


def softplus(v):
    e = jnp.exp(-jnp.abs(v))
    r = 1.0 / (1.0 + e)
    return jnp.maximum(v, 0.0) + jnp.log1p(e), jnp.where(v >= 0.0, r, e * r)


def halves(v):
    high = v.astype(BF)
    return high, (v - high.astype(F4)).astype(BF)


def masks():
    col = lax.broadcasted_iota(jnp.int32, (ROWS_STEP, SUB * NS), 1)
    row = lax.broadcasted_iota(jnp.int32, (ROWS_STEP, SUB * NS), 0)
    state = lax.broadcasted_iota(jnp.int32, (NS, SUB * NS), 0)
    state_col = lax.broadcasted_iota(jnp.int32, (NS, SUB * NS), 1)
    tiled = jnp.where(state_col % NS == state, 1.0, 0.0).astype(BF)
    return col // NS == row % SUB, tiled


def diagonals(values, own, tiled, out):
    for part, v in enumerate(halves(values)):
        out[part] = jnp.where(own, nn(v, tiled), 0.0).astype(BF).reshape(SUBS, SUB, SUB * NS)


def diagonal(diag, s):
    return jnp.concatenate([diag[0, s], diag[1, s]], axis=0)


def folded(values, own, tiled):
    high, low = halves(jnp.where(own, values, 0.0))
    return nt(high, tiled) + nt(low, tiled)


def columns_of(bct, bc):
    turned = jnp.concatenate([bc, jnp.zeros((ROWS_STEP, 128 - 2 * NS), F4)], axis=1).T
    for s in range(SUBS):
        bct[s] = turned[0 : 2 * NS, s * SUB : (s + 1) * SUB]


def scan_kernel(pf, u_in, z, *refs):
    ps, refs = refs[:PER_STEP], refs[PER_STEP:]
    (dtw, dtb, rates, skip, y, gated, d_out, slope_out, marks, *scratch) = refs
    state, dbuf, wbuf, hb0, hb1, bct, diag = scratch
    r = pl.program_id(0)

    @pl.when(r == 0)
    def _():
        state[...] = jnp.zeros_like(state)

    proj = joined(ps)
    low = proj[:, :R].astype(BF)
    v = jnp.concatenate(
        [nn(low[own_runs(s)], dtw[pf[O_KIND + r * PER_STEP + s]]) for s in range(PER_STEP)], axis=0
    )
    delta, slope = softplus(v + dtb[...])
    slope_out[...] = slope
    d_out[...] = delta
    u = u_in[...]
    dbuf[...] = delta
    wbuf[...] = delta * u
    y[...] = skip[...] * u
    rate = rates[...]
    columns_of(bct, proj[:, R:])
    diagonals(proj[:, R + NS :], *masks(), diag)

    def advance(s, h, hb):
        base = pl.multiple_of(s * SUB, SUB)
        marks[s] = h
        d_rows = dbuf[pl.ds(base, SUB), :]
        w_rows = wbuf[pl.ds(base, SUB), :]
        b_cols = bct[s]
        for i in range(SUB):
            a = jnp.exp2(d_rows[i : i + 1, :] * rate)
            h = a * h + b_cols[0:NS, i : i + 1] * w_rows[i : i + 1, :]
            hb[i * NS : (i + 1) * NS, :] = h.astype(BF)
        return h

    def sums(s, hb):
        both = nn(diagonal(diag, s), hb[...])
        y[pl.ds(pl.multiple_of(s * SUB, SUB), SUB), :] += both[0:SUB] + both[SUB:]

    def pair(k, h):
        sums(2 * k, hb0)
        h = advance(2 * k + 1, h, hb1)
        sums(2 * k + 1, hb1)
        return advance(2 * k + 2, h, hb0)

    h = advance(0, state[...], hb0)
    h = lax.fori_loop(0, SUBS // 2 - 1, pair, h)
    sums(SUBS - 2, hb0)
    state[...] = advance(SUBS - 1, h, hb1)
    sums(SUBS - 1, hb1)
    zf = z[...].astype(F4)
    gated[...] = (y[...] * (zf * jax.nn.sigmoid(zf))).astype(BF)


def scan_call(pf, u, z, proj, dtw, dtb, rates, skip):
    return pl.pallas_call(
        scan_kernel,
        out_shape=[
            pltpu.HBM((LEN, EC), F4),
            jax.ShapeDtypeStruct((LEN, EC), BF),
            pltpu.HBM((LEN, EC), F4),
            pltpu.HBM((LEN, EC), F4),
            pltpu.HBM((LEN // SUB, NS, EC), F4),
        ],
        grid_spec=pltpu.PrefetchScalarGridSpec(
            num_scalar_prefetch=1,
            grid=(STEPS,),
            in_specs=[step_spec(EC), step_spec(EC)]
            + pos_specs(PROJ)
            + [whole((MODES, R, EC)), whole((1, EC)), whole((NS, EC)), whole((1, EC))],
            out_specs=[
                step_spec(EC),
                step_spec(EC),
                step_spec(EC),
                step_spec(EC),
                pl.BlockSpec((SUBS, NS, EC), lambda i, pf: (i, 0, 0)),
            ],
            scratch_shapes=[
                pltpu.VMEM((NS, EC), F4),
                pltpu.VMEM((ROWS_STEP, EC), F4),
                pltpu.VMEM((ROWS_STEP, EC), F4),
                pltpu.VMEM((SUB * NS, EC), BF),
                pltpu.VMEM((SUB * NS, EC), BF),
                pltpu.VMEM((SUBS, 2 * NS, SUB), F4),
                pltpu.VMEM((2, SUBS, SUB, SUB * NS), BF),
            ],
        ),
        compiler_params=params(20),
        cost_estimate=cost(1 << 29, 12 << 20, 9 << 20),
        name="scan_forward",
    )(pf, u, z, *[proj] * PER_STEP, dtw, dtb, rates, skip)


def back_kernel(pf, u_in, d_in, slope, gg, z, y_in, *refs):
    ps, refs = refs[:PER_STEP], refs[PER_STEP:]
    (dtw, marks, rates, skip, usg, zgrad, near, far, dt_tail, alog, dtbg, skipg, *scratch) = refs
    (carry, dtwg, hprev, gb0, rb0, pb0, pc0, gb1, rb1, pb1, pc1, *scratch) = scratch
    wbuf, ybuf, pbuf, bct, diag, cbuf, bbuf, part = scratch
    r = pl.program_id(0)

    @pl.when(r == 0)
    def _():
        carry[...] = jnp.zeros_like(carry)
        dtwg[...] = jnp.zeros_like(dtwg)
        alog[...] = jnp.zeros_like(alog)
        dtbg[...] = jnp.zeros_like(dtbg)
        skipg[...] = jnp.zeros_like(skipg)

    delta = d_in[...]
    u = u_in[...]
    zf = z[...].astype(F4)
    q = jax.nn.sigmoid(zf)
    gf = gg[...].astype(F4)
    yg = gf * (zf * q)
    zgrad[...] = (gf * y_in[...] * (q * (1.0 + zf * (1.0 - q)))).astype(BF)
    wbuf[...] = delta * u
    ybuf[...] = yg
    skipg[...] += jnp.sum(yg * u, axis=0, keepdims=True)
    rate = rates[...]
    proj = joined(ps)
    columns_of(bct, proj[:, R:])
    own, tiled = masks()
    diagonals(proj[:, R : R + NS], own, tiled, diag)

    ones = jnp.where(own[:SUB], 1.0, 0.0).astype(BF)

    def lanes(v):
        return (v[:, 0:128] + v[:, 128:256]) + (v[:, 256:384] + v[:, 384:512])

    def retreat(s, carried, bufs):
        gb, rb, pb, pc = bufs
        ag, al = carried
        base = pl.multiple_of(s * SUB, SUB)
        d_rows = d_in[pl.ds(base, SUB), :]
        w_rows = wbuf[pl.ds(base, SUB), :]
        y_rows = ybuf[pl.ds(base, SUB), :]
        bc_cols = bct[s]
        h = marks[s]
        for i in range(SUB):
            hprev[i] = h
            a = jnp.exp2(d_rows[i : i + 1, :] * rate)
            h = a * h + bc_cols[0:NS, i : i + 1] * w_rows[i : i + 1, :]
            pc[i * NS : (i + 1) * NS, :] = lanes(h * y_rows[i : i + 1, :]).astype(BF)
        for i in reversed(range(SUB)):
            g = ag + bc_cols[NS:, i : i + 1] * y_rows[i : i + 1, :]
            gb[i * NS : (i + 1) * NS, :] = g.astype(BF)
            pb[i * NS : (i + 1) * NS, :] = lanes(g * w_rows[i : i + 1, :]).astype(BF)
            ag = jnp.exp2(d_rows[i : i + 1, :] * rate) * g
            rp = rate * (ag * hprev[i])
            rb[i * NS : (i + 1) * NS, :] = rp.astype(BF)
            al = al + d_rows[i : i + 1, :] * rp
        return ag, al

    full = jnp.ones((SUB, 128), BF)

    def sums(s, bufs):
        gb, rb, pb, pc = bufs
        at = pl.ds(pl.multiple_of(s * SUB, SUB), SUB)
        both = nn(diagonal(diag, s), gb[...])
        bsum = both[0:SUB] + both[SUB:]
        dsum = nn(ones, rb[...])
        cbuf[at, :] = nt(full, pc[...])
        bbuf[at, :] = nt(full, pb[...])
        usg[at, :] = d_in[at, :] * bsum + skip[...] * ybuf[at, :]
        pbuf[at, :] = dsum * LN2 + u_in[at, :] * bsum

    even, odd = (gb0, rb0, pb0, pc0), (gb1, rb1, pb1, pc1)

    def pair(k, carried):
        s = SUBS - 1 - 2 * k
        sums(s, even)
        carried = retreat(s - 1, carried, odd)
        sums(s - 1, odd)
        return retreat(s - 2, carried, even)

    carried = retreat(SUBS - 1, (carry[...], jnp.zeros((NS, EC), F4)), even)
    carried = lax.fori_loop(0, SUBS // 2 - 1, pair, carried)
    sums(1, even)
    ag, al = retreat(0, carried, odd)
    sums(0, odd)
    carry[...] = ag
    alog[...] += al * LN2
    pre = pbuf[...] * slope[...]
    dtbg[...] += jnp.sum(pre, axis=0, keepdims=True)
    pre_low = pre.astype(BF)
    bgrad = folded(bbuf[...], own, tiled)
    cgrad = folded(cbuf[...], own, tiled)
    low = proj[:, :R].astype(BF)
    for s in range(PER_STEP):
        run = (STEPS - 1 - r) * PER_STEP + s
        kind = pf[O_KIND + run]
        at = pl.ds(pl.multiple_of(pf[O_POS + run] * RUN, RUN), RUN)
        part[at, :R] = nt(pre_low[own_runs(s)], dtw[kind])
        part[at, R : R + NS] = bgrad[own_runs(s)]
        part[at, R + NS :] = cgrad[own_runs(s)]
        dtwg[kind] += tn(low[own_runs(s)], pre_low[own_runs(s)])

    @pl.when(r == STEPS - 1)
    def _():
        near[...] = part[: LEN // 2, :]
        far[...] = part[LEN // 2 :, :]
        for s in range(16):
            for m in range(MODES):
                dt_tail[s, m * 8 : (m + 1) * 8, :] = dtwg[m, s * 8 : (s + 1) * 8, :]


def back_call(pf, u, delta, slope, gg, z, y, proj, dtw, marks, rates, skip):
    return pl.pallas_call(
        back_kernel,
        out_shape=[
            jax.ShapeDtypeStruct((LEN, EC), F4),
            jax.ShapeDtypeStruct((LEN, EC), BF),
            jax.ShapeDtypeStruct((LEN // 2, PROJ), F4),
            jax.ShapeDtypeStruct((LEN // 2, PROJ), F4),
            jax.ShapeDtypeStruct((16, MODES * 8, EC), F4),
            jax.ShapeDtypeStruct((NS, EC), F4),
            jax.ShapeDtypeStruct((1, EC), F4),
            jax.ShapeDtypeStruct((1, EC), F4),
        ],
        grid_spec=pltpu.PrefetchScalarGridSpec(
            num_scalar_prefetch=1,
            grid=(STEPS,),
            in_specs=[step_spec(EC, True)] * 6
            + pos_specs(PROJ, True)
            + [
                whole((MODES, R, EC)),
                pl.BlockSpec((SUBS, NS, EC), lambda i, pf: (STEPS - 1 - i, 0, 0)),
                whole((NS, EC)),
                whole((1, EC)),
            ],
            out_specs=[
                step_spec(EC, True),
                step_spec(EC, True),
                whole((LEN // 2, PROJ)),
                whole((LEN // 2, PROJ)),
                whole((16, MODES * 8, EC)),
                whole((NS, EC)),
                whole((1, EC)),
                whole((1, EC)),
            ],
            scratch_shapes=[
                pltpu.VMEM((NS, EC), F4),
                pltpu.VMEM((MODES, R, EC), F4),
                pltpu.VMEM((SUB, NS, EC), F4),
                *([pltpu.VMEM((SUB * NS, EC), BF)] * 2 + [pltpu.VMEM((SUB * NS, 128), BF)] * 2) * 2,
                pltpu.VMEM((ROWS_STEP, EC), F4),
                pltpu.VMEM((ROWS_STEP, EC), F4),
                pltpu.VMEM((ROWS_STEP, EC), F4),
                pltpu.VMEM((SUBS, 2 * NS, SUB), F4),
                pltpu.VMEM((2, SUBS, SUB, SUB * NS), BF),
                pltpu.VMEM((ROWS_STEP, SUB * NS), F4),
                pltpu.VMEM((ROWS_STEP, SUB * NS), F4),
                pltpu.VMEM((LEN, PROJ), F4),
            ],
        ),
        compiler_params=params(24),
        cost_estimate=cost(1 << 30, 14 << 20, 9 << 20),
        name="scan_backward",
    )(pf, u, delta, slope, gg, z, y, *[proj] * PER_STEP, dtw, marks, rates, skip)


def conv_back_kernel(pf, *refs):
    pgs, refs = refs[:PER_STEP], refs[PER_STEP:]
    (xw, usg, u, slope, x_now, x_before, taps, out, x_tail, cwg, cbg, gbuf, xbuf, xwg) = refs
    r = pl.program_id(0)

    @pl.when(r == 0)
    def _():
        xwg[...] = jnp.zeros_like(xwg)
        cwg[...] = jnp.zeros_like(cwg)
        cbg[...] = jnp.zeros_like(cbg)
        gbuf[ROWS_STEP:, :] = jnp.zeros((8, EC), F4)

    @pl.when(r > 0)
    def _():
        gbuf[ROWS_STEP:, :] = gbuf[0:8, :]

    u_low = u[...].astype(BF)
    kinds = [pf[O_KIND + (STEPS - 1 - r) * PER_STEP + s] for s in range(PER_STEP)]
    u_grad = usg[...] + jnp.concatenate([nn(pgs[s][...], xw[kinds[s]]) for s in range(PER_STEP)], axis=0)
    grad = u_grad * slope[...]
    gbuf[0:ROWS_STEP, :] = grad
    cbg[...] += jnp.sum(grad, axis=0, keepdims=True)
    before = x_before[...].astype(F4)[16 - 8 :, :]
    xbuf[0:8, :] = jnp.where(r == STEPS - 1, jnp.zeros_like(before), before)
    xbuf[8:, :] = x_now[...].astype(F4)
    back = taps[KC - 1 : KC, :] * grad
    for i in range(KC):
        cwg[i : i + 1, :] += jnp.sum(grad * xbuf[5 + i : 5 + i + ROWS_STEP, :], axis=0, keepdims=True)
        if i < KC - 1:
            back = back + taps[i : i + 1, :] * gbuf[KC - 1 - i : KC - 1 - i + ROWS_STEP, :]
    out[...] = back.astype(BF)
    for s in range(PER_STEP):
        xwg[kinds[s]] += tn(pgs[s][...], u_low[own_runs(s)])

    @pl.when(r == STEPS - 1)
    def _():
        for s in range(16):
            for m in range(MODES):
                x_tail[s, m * 10 : (m + 1) * 10, :] = xwg[m, s * 10 : (s + 1) * 10, :]
            x_tail[s, MODES * 10 :, :] = jnp.zeros((TAIL_OUT - 24 - MODES * 10, EC), F4)


def conv_back_call(pf, pg, xw, usg, u, slope, x_pre, taps):
    before = ROWS_STEP // 16
    return pl.pallas_call(
        conv_back_kernel,
        out_shape=[
            jax.ShapeDtypeStruct((LEN, EC), BF),
            jax.ShapeDtypeStruct((16, TAIL_OUT - 24, EC), F4),
            jax.ShapeDtypeStruct((KC, EC), F4),
            jax.ShapeDtypeStruct((1, EC), F4),
        ],
        grid_spec=pltpu.PrefetchScalarGridSpec(
            num_scalar_prefetch=1,
            grid=(STEPS,),
            in_specs=pos_specs(PROJ, True)
            + [
                whole((MODES, PROJ, EC)),
                step_spec(EC, True),
                step_spec(EC, True),
                step_spec(EC, True),
                step_spec(EC, True),
                pl.BlockSpec(
                    (16, EC), lambda i, pf: (jnp.maximum((STEPS - 1 - i) * before - 1, 0), 0)
                ),
                whole((KC, EC)),
            ],
            out_specs=[
                step_spec(EC, True),
                whole((16, TAIL_OUT - 24, EC)),
                whole((KC, EC)),
                whole((1, EC)),
            ],
            scratch_shapes=[
                pltpu.VMEM((ROWS_STEP + 8, EC), F4),
                pltpu.VMEM((ROWS_STEP + 8, EC), F4),
                pltpu.VMEM((MODES, PROJ, EC), F4),
            ],
        ),
        compiler_params=params(16),
        cost_estimate=cost(1 << 29, 8 << 20, 1 << 20),
        name="conv_backward",
    )(pf, *[pg] * PER_STEP, xw, usg, u, slope, x_pre, x_pre, taps)


def ring(v, axis, step):
    return lax.ppermute(v, axis, [(i, (i + step) % 4) for i in range(4)])


def across(v):
    return lax.ppermute(v, "c", [(0, 1), (1, 0)])


def after(value, *others):
    return lax.optimization_barrier((value, others))[0]


def add(*values):
    total = values[0].astype(F4)
    for value in values[1:]:
        total = total + value.astype(F4)
    return total


def spread_chan(rows):
    left = ring(rows, "y", 1)
    right = ring(rows, "y", -1)
    far = [ring(left[:RUN], "y", 1), ring(right[RUN:], "y", -1)]
    near = jnp.concatenate([rows, right, *far, left], axis=0)
    return jnp.concatenate([near, across(near)], axis=0)


def collect_chan(near, far):
    pair = add(near, across(far)).astype(BF).reshape(4, 2 * RUN, D)
    own, right, far_first, far_second, left = pair[0], pair[1], pair[2, :RUN], pair[2, RUN:], pair[3]
    came = ring(far_first, "y", 1)
    came_back = ring(far_second, "y", -1)
    right = jnp.concatenate([add(right[:RUN], came).astype(BF), right[RUN:]], axis=0)
    left = jnp.concatenate([left[:RUN], add(left[RUN:], came_back).astype(BF)], axis=0)
    return add(own, ring(right, "y", 1), ring(left, "y", -1))


def direct(v, axis):
    return [v, ring(v, axis, -1), ring(v, axis, 2), ring(v, axis, 1)]


def sum_chan(near, far, finish, fill=None):
    pair = add(near, across(far)).reshape(4, LEN // 8, near.shape[1])
    came = [ring(pair[1], "y", 1), ring(pair[2], "y", 2), ring(pair[3], "y", -1)]
    filled = None
    if fill:
        filled = fill(pair)
        came = after(came, filled)
    mine = jnp.concatenate(direct(finish(add(pair[0], *came)), "y"), axis=0)
    return jnp.concatenate([mine, across(mine)], axis=0), filled


def sum_axis(v, axis):
    v = jnp.roll(v, -lax.axis_index(axis), 0)
    return add(v[0], ring(v[1], axis, 1), ring(v[2], axis, 2), ring(v[3], axis, -1))


def sum_pair(v):
    place = lax.axis_index("c")
    keep = lax.dynamic_index_in_dim(v, place, 2, False)
    give = lax.dynamic_index_in_dim(v, 1 - place, 2, False)
    return sum_axis(jnp.swapaxes(keep + across(give), 0, 1), "y")


def sum_seq(v):
    return sum_axis(sum_axis(v.reshape(4, 4, v.shape[1]), "z"), "x")


def local(
    layer_input, kinds, norm_gain, in_weight, conv_weight, conv_bias, x_weight, dt_weight,
    dt_bias, a_log, d_skip, out_weight, cotangent,
):
    place_y, place_c = lax.axis_index("y"), lax.axis_index("c")
    chan = place_y * 2 + place_c
    gain = norm_gain.astype(F4)
    taps = conv_weight.astype(F4)
    cbias = conv_bias.astype(F4)[None, :]
    dtb = dt_bias.astype(F4)[None, :]
    a_own = lax.dynamic_slice_in_dim(a_log, chan * EC, EC, 1).astype(F4)
    rates = -jnp.exp(a_own) * LOG2E
    skip = lax.dynamic_slice_in_dim(d_skip, chan * EC, EC, 0).astype(F4)[None, :]

    x32 = layer_input.astype(F4)
    rms = lax.rsqrt(jnp.mean(x32 * x32, axis=1, keepdims=True) + 1e-05)
    normed = (x32 * rms * gain[None, :]).astype(BF)

    early_w = lax.all_gather(
        jnp.concatenate(
            [
                in_weight[:, :, 0, :].reshape(ROWS, EC),
                in_weight[:, :, 1, :].reshape(ROWS, EC),
                jnp.concatenate([x_weight, dt_weight[:, :6]], axis=1).reshape(48, EC),
                jnp.pad(dt_weight[:, 6:].reshape(6, EC), ((0, 10), (0, 0))),
            ],
            axis=0,
        ),
        SEQ,
    )
    pf = slot_plan(kinds)
    xs = spread_chan(normed)
    cs = spread_chan(cotangent)
    out_w = lax.all_gather(after(out_weight.reshape(ROWS, EC), xs, cs), SEQ)
    rates, skip, taps, cbias, dtb, xs = after((rates, skip, taps, cbias, dtb, xs), pf)
    early_w = after(early_w, rates, skip, taps, cbias, dtb, xs)
    x_pre = down(pf, in_hbm(xs), early_w, "project_scan")
    u, conv_slope, near, far, xw, dtw = conv_call(pf, x_pre, taps, cbias, early_w, 2 * ROWS)
    proj, z = sum_chan(
        near,
        far,
        lambda total: total,
        lambda pair: down(after(pf, pair), xs, early_w, "project_gate", MODES),
    )
    y, gated, delta, slope, marks = scan_call(pf, u, z, proj, dtw, dtb, rates, skip)

    out_part = outer(pf, "out_weight_grad", cs, gated, ROWS)
    out_sum = lax.psum_scatter(out_part, SEQ, scatter_dimension=0).astype(F4)
    gg = down(after(pf, out_part), in_hbm(cs), out_w, "project_cotangent")
    usg, zgrad, near, far, dt_tail, alog, dtbg, skipg = back_call(
        pf, u, delta, slope, gg, z, y, proj, dtw, marks, rates, skip
    )
    pg, weights_part = sum_chan(
        near,
        far,
        lambda total: total.astype(BF),
        lambda pair: outer(after(pf, pair), "gate_weight_grad", xs, zgrad, 2 * ROWS + TAIL_OUT),
    )
    xgrad, x_tail, cwg, cbg = conv_back_call(pf, pg, xw, usg, u, conv_slope, x_pre, taps)
    weights_part = outer(
        after(pf, out_sum),
        "scan_weight_grad",
        xs,
        xgrad,
        2 * ROWS + TAIL_OUT,
        ROWS,
        weights_part,
        (dt_tail, x_tail),
    )
    in_grad, x_w_grad, dt_w_grad = unpack(lax.psum_scatter(weights_part, SEQ, scatter_dimension=0))

    pf = after(pf, weights_part)
    branch = collect_chan(*up(pf, "project_out", (gated, out_w, 0)))
    mixed = (x32 + branch).astype(BF)
    near, far, gain_part = up(
        pf, "input_grad", (xgrad, early_w, 0), (zgrad, early_w, MODES), xs=xs
    )
    ngrad = collect_chan(near, far) * gain[None, :]
    x_grad = (
        cotangent.astype(F4)
        + rms * ngrad
        - x32 * (rms * rms * rms) * jnp.mean(ngrad * x32, axis=1, keepdims=True)
    )
    out_grad = out_sum.reshape(MODES, 128, EC)
    gain_part = sum_pair((gain_part[0] / gain).reshape(16, 4, 2, 16))
    small = jnp.concatenate([cwg, cbg, dtbg, skipg, alog], axis=0)
    small = jnp.swapaxes(small.reshape(23, 16, 32), 0, 1).reshape(16, 23 * 32)
    small = sum_seq(jnp.concatenate([small, gain_part, jnp.zeros((16, 16), F4)], axis=1))
    gain_grad = small[23 * 32 : 24 * 32 - 16]
    moves = [(s * 8 + c, c * 16 + s) for s in range(16) for c in range(8)]
    own = lax.ppermute(small[: 23 * 32].reshape(23, 32), ("z", "x", "y", "c"), moves)
    return (
        mixed,
        x_grad,
        gain_grad,
        in_grad,
        own[0:4],
        own[4],
        x_w_grad,
        dt_w_grad,
        own[5],
        own[7:],
        own[6],
        out_grad,
    )


def solution(mesh):
    fine = Mesh(mesh.devices.reshape(4, 4, 4, 2), ("z", "x", "y", "c"))
    rows = ("z", "x", "y", "c")
    return jax.shard_map(
        local,
        mesh=fine,
        in_specs=(
            P(rows, None),
            P(SEQ),
            P(),
            P(None, SEQ, None, CHAN),
            P(None, CHAN),
            P(CHAN),
            P(None, SEQ, CHAN),
            P(None, SEQ, CHAN),
            P(CHAN),
            P(),
            P(),
            P(None, SEQ, CHAN),
            P(rows, None),
        ),
        out_specs=(
            P(rows, None),
            P(rows, None),
            P(rows),
            P(None, SEQ, None, CHAN),
            P(None, rows),
            P(rows),
            P(None, SEQ, CHAN),
            P(None, SEQ, CHAN),
            P(rows),
            P(None, rows),
            P(rows),
            P(None, SEQ, CHAN),
        ),
        check_vma=False,
    )
```

```python
import functools

import jax
import jax.numpy as jnp
import numpy as np
from jax import lax
from jax.experimental import pallas as pl
from jax.experimental.pallas import tpu as pltpu
from jax.sharding import Mesh
from jax.sharding import PartitionSpec as P

NS = 16
KC = 4
R = 128
MODES = 3
RUN = 64
RUNS = 16
LEN = 1024
D = 2048
EC = 512
PER = 4
BLK = RUN * PER
NBLK = 6
SLOTS = NBLK * PER
SUB = 16
NSUB = RUN // SUB
LOG2E = 1.4426950408889634
LN2 = 0.6931471805599453
ROWS = MODES * 128
TAIL_IN = 64
TAIL_OUT = 64
PROJ = R + 2 * NS

BF = jnp.bfloat16
F4 = jnp.float32

O_RUN = 0
O_VALID = SLOTS
O_PLACE = 2 * SLOTS
O_BK = 3 * SLOTS
O_TOTAL = O_BK + NBLK
O_KIND = O_TOTAL + 1
O_POS = O_KIND + RUNS
O_FIRST = O_POS + RUNS
O_COUNT = O_FIRST + MODES

SEQ = ("z", "x")
CHAN = ("y", "c")


def params(limit=56):
    return pltpu.CompilerParams(vmem_limit_bytes=limit << 20)


def in_hbm(x):
    return pltpu.with_memory_space_constraint(x, pltpu.HBM)


def cost(flops, moved, trans=0):
    return pl.CostEstimate(flops=int(flops), bytes_accessed=int(moved), transcendentals=int(trans))


def nt(a, b):
    return lax.dot_general(a, b, (((1,), (1,)), ((), ())), preferred_element_type=F4)


def tn(a, b):
    return lax.dot_general(a, b, (((0,), (0,)), ((), ())), preferred_element_type=F4)


def nn(a, b):
    return jnp.dot(a, b, preferred_element_type=F4)


def whole(shape):
    zeros = (0,) * len(shape)
    return pl.BlockSpec(shape, lambda i, pf: zeros)


def slot_plan(kinds):
    me_y, me_c = lax.axis_index("y"), lax.axis_index("c")
    run_kind = kinds.reshape(RUNS, RUN)[:, 0]
    one_hot = (run_kind[:, None] == jnp.arange(MODES, dtype=jnp.int32)[None, :]).astype(jnp.int32)
    count = jnp.sum(one_hot, axis=0)
    blocks = (count + PER - 1) // PER
    first = jnp.cumsum(blocks) - blocks
    rank = jnp.cumsum(one_hot, axis=0) - one_hot
    slot = jnp.sum(one_hot * (PER * first[None, :] + rank), axis=1)
    slots = jnp.arange(SLOTS, dtype=jnp.int32)
    hit = (slot[None, :] == slots[:, None]).astype(jnp.int32)
    valid = jnp.sum(hit, axis=1)
    head = (slot[None, :] == (slots // PER * PER)[:, None]).astype(jnp.int32)
    runs = jnp.arange(RUNS, dtype=jnp.int32)
    run_of = jnp.sum(jnp.where(valid[:, None] > 0, hit, head) * runs[None, :], axis=1)
    total = jnp.sum(blocks)
    place = jnp.minimum(jnp.arange(NBLK, dtype=jnp.int32), total - 1)
    block_kind = jnp.sum((place[:, None] >= first[None, 1:]).astype(jnp.int32), axis=1)

    def position(run):
        core = jnp.where((run // 2) % 2 == me_c, 0, 1)
        return core * 8 + ((run // 4 - me_y) % 4) * 2 + run % 2

    return jnp.concatenate(
        [
            run_of,
            valid,
            position(run_of),
            block_kind,
            total[None],
            run_kind,
            position(runs),
            first,
            blocks,
        ]
    ).astype(jnp.int32)


def slot_run(pf, b, s):
    return pl.multiple_of(pf[O_RUN + b * PER + s] * RUN, RUN)


def slot_place(pf, b, s):
    return pl.multiple_of(pf[O_PLACE + b * PER + s] * RUN, RUN)


def live(i, pf):
    return jnp.minimum(i, pf[O_TOTAL] - 1)


def seq_spec(first):
    return pl.BlockSpec((16, 128, EC), lambda i, pf: (0, first + pf[O_BK + i], 0))


def row_specs():
    def one(s):
        return pl.BlockSpec((RUN, D), lambda i, pf: (pf[O_PLACE + live(i, pf) * PER + s], 0))

    return [one(s) for s in range(PER)]


def down_kernel(pf, x0, x1, x2, x3, w, out):
    b = pl.program_id(0)

    @pl.when(b < pf[O_TOTAL])
    def _():
        rows = jnp.concatenate([x0[...], x1[...], x2[...], x3[...]], axis=0)
        value = nn(rows, w[...].reshape(D, EC)).astype(BF)
        for s in range(PER):
            out[pl.ds(slot_run(pf, b, s), RUN), :] = value[s * RUN : (s + 1) * RUN]


def down(pf, x, w, name, first=0):
    return pl.pallas_call(
        down_kernel,
        out_shape=jax.ShapeDtypeStruct((LEN, EC), BF),
        grid_spec=pltpu.PrefetchScalarGridSpec(
            num_scalar_prefetch=1,
            grid=(NBLK,),
            in_specs=row_specs() + [seq_spec(first)],
            out_specs=whole((LEN, EC)),
        ),
        compiler_params=params(16),
        cost_estimate=cost(6 * 2 * BLK * D * EC, 14 << 20),
        name=name,
    )(pf, x, x, x, x, in_hbm(w))


def up_kernel(pf, *refs, pairs, with_gain):
    if with_gain:
        xs = refs[2 * pairs : 2 * pairs + PER]
        near, far, gain, both = refs[2 * pairs + PER :]
    else:
        near, far, both = refs[2 * pairs :]
    b = pl.program_id(0)

    if with_gain:

        @pl.when(b == 0)
        def _():
            gain[...] = jnp.zeros_like(gain)

    @pl.when(b < pf[O_TOTAL])
    def _():
        tile = None
        for p in range(pairs):
            g, w = refs[2 * p], refs[2 * p + 1]
            rows = jnp.concatenate([g[pl.ds(slot_run(pf, b, s), RUN), :] for s in range(PER)], axis=0)
            term = nt(rows, w[...].reshape(D, EC))
            tile = term if p == 0 else tile + term
        for s in range(PER):
            part = tile[s * RUN : (s + 1) * RUN]
            both[pl.ds(slot_place(pf, b, s), RUN), :] = part.astype(BF)
            if with_gain:
                term = jnp.sum(part * xs[s][...].astype(F4), axis=0, keepdims=True)
                gain[...] += jnp.where(pf[O_VALID + b * PER + s] > 0, term, jnp.zeros_like(term))

    @pl.when(b == NBLK - 1)
    def _():
        near[...] = both[: LEN // 2, :]
        far[...] = both[LEN // 2 :, :]


def up(pf, name, *terms, xs=None):
    side = whole((LEN // 2, D))
    args, specs = [], []
    for g, w, first in terms:
        args += [g, in_hbm(w)]
        specs += [whole((LEN, EC)), seq_spec(first)]
    out_shape, out_specs = [pltpu.HBM((LEN // 2, D), BF)] * 2, [side] * 2
    if xs is not None:
        args += [in_hbm(xs)] * PER
        specs += row_specs()
        out_shape = out_shape + [jax.ShapeDtypeStruct((1, D), F4)]
        out_specs = out_specs + [whole((1, D))]
    return pl.pallas_call(
        functools.partial(up_kernel, pairs=len(terms), with_gain=xs is not None),
        out_shape=out_shape,
        grid_spec=pltpu.PrefetchScalarGridSpec(
            num_scalar_prefetch=1,
            grid=(NBLK,),
            in_specs=specs,
            out_specs=out_specs,
            scratch_shapes=[pltpu.VMEM((LEN, D), BF)],
        ),
        compiler_params=params(32),
        cost_estimate=cost(len(terms) * 6 * 2 * BLK * D * EC, 14 << 20),
        name=name,
    )(pf, *args)


def outer_kernel(pf, x_in, g_in, *refs, tail):
    out, sorted_g = refs[-2:]

    @pl.when(pl.program_id(0) == 0)
    def _():
        for b in range(NBLK):
            for s in range(PER):
                rows = g_in[pl.ds(slot_run(pf, b, s), RUN), :]
                rows = jnp.where(pf[O_VALID + b * PER + s] > 0, rows, jnp.zeros_like(rows))
                at = b * BLK + s * RUN
                sorted_g[at : at + RUN, :] = rows

    def one_kind(m, carry):
        first, count = pf[O_FIRST + m], pf[O_COUNT + m]
        rows = pl.ds(pl.multiple_of(m * 128, 128), 128)

        @pl.when(count == 0)
        def _():
            for s in range(4):
                out[s, rows, :] = jnp.zeros((128, EC), BF)

        for n in range(1, RUNS // PER + 1):

            @pl.when(count == n)
            def _():
                x = jnp.concatenate(
                    [x_in[pl.ds(slot_place(pf, first, s), RUN), :] for s in range(n * PER)], axis=0
                )
                g = sorted_g[pl.ds(pl.multiple_of(first * BLK, BLK), n * BLK), :]
                value = tn(x, g).astype(BF)
                for s in range(4):
                    out[s, rows, :] = value[s * 128 : (s + 1) * 128, :]

        return carry

    lax.fori_loop(0, MODES, one_kind, 0)
    if tail:
        dt_tail, x_tail = refs[:2]
        for s in range(4):
            out[s, ROWS:, :] = jnp.concatenate([dt_tail[s], x_tail[s]], axis=0).astype(BF)


def outer(pf, name, x, g, held_rows, first=0, held=None, tails=()):
    rows = ROWS + (TAIL_OUT if tails else 0)
    specs = [pl.BlockSpec((LEN, 512), lambda i, pf: (0, i)), whole((LEN, EC))]
    args = [x, g]
    if tails:
        specs += [
            pl.BlockSpec((4, 24, EC), lambda i, pf: (i, 0, 0)),
            pl.BlockSpec((4, TAIL_OUT - 24, EC), lambda i, pf: (i, 0, 0)),
        ]
        args += tails
    aliases = {}
    if held is not None:
        specs.append(pl.BlockSpec(memory_space=pl.ANY))
        args.append(held)
        aliases = {len(args): 0}
    if first % rows == 0:
        out_spec = pl.BlockSpec((4, rows, EC), lambda i, pf: (i, first // rows, 0))
    else:
        out_spec = pl.BlockSpec((pl.Element(4), pl.Element(rows), pl.Element(EC)), lambda i, pf: (4 * i, first, 0))
    return pl.pallas_call(
        functools.partial(outer_kernel, tail=bool(tails)),
        out_shape=pltpu.HBM((16, held_rows, EC), BF),
        grid_spec=pltpu.PrefetchScalarGridSpec(
            num_scalar_prefetch=1,
            grid=(4,),
            in_specs=specs,
            out_specs=out_spec,
            scratch_shapes=[pltpu.VMEM((NBLK * BLK, EC), BF)],
        ),
        input_output_aliases=aliases,
        compiler_params=params(20),
        cost_estimate=cost(6 * 2 * BLK * D * EC, 14 << 20),
        name=name,
    )(pf, *args)


def unpack_kernel(scan, gate, tail, in_grad, x_w_grad, dt_w_grad):
    in_grad[0, :, 0, :] = scan[...].astype(F4)
    in_grad[0, :, 1, :] = gate[...].astype(F4)

    @pl.when(pl.program_id(0) == 0)
    def _():
        rows = tail[...].astype(F4)
        for m in range(MODES):
            dt_w_grad[m] = rows[m * 8 : (m + 1) * 8]
            x_w_grad[:, m, :] = rows[24 + m * 10 : 24 + (m + 1) * 10]


def unpack(sums):
    sums = in_hbm(sums)
    in_grad, x_w_grad, dt_w_grad = pl.pallas_call(
        unpack_kernel,
        grid=(MODES,),
        in_specs=[
            pl.BlockSpec((128, EC), lambda m: (MODES + m, 0)),
            pl.BlockSpec((128, EC), lambda m: (m, 0)),
            pl.BlockSpec((TAIL_OUT, EC), lambda m: (2 * ROWS // TAIL_OUT, 0)),
        ],
        out_specs=[
            pl.BlockSpec((1, 128, 2, EC), lambda m: (m, 0, 0, 0)),
            pl.BlockSpec((10, MODES, EC), lambda m: (0, 0, 0)),
            pl.BlockSpec((MODES, 8, EC), lambda m: (0, 0, 0)),
        ],
        out_shape=[
            jax.ShapeDtypeStruct((MODES, 128, 2, EC), F4),
            jax.ShapeDtypeStruct((10, MODES, EC), F4),
            jax.ShapeDtypeStruct((MODES, 8, EC), F4),
        ],
        compiler_params=params(12),
        cost_estimate=cost(0, 3 << 20),
        name="unpack_sums",
    )(sums, sums, sums)
    return in_grad, jnp.swapaxes(x_w_grad, 0, 1), dt_w_grad


def pickers():
    col = np.arange(256)[None, :]
    i = np.arange(PROJ)[:, None]
    k = np.arange(R)[:, None]
    slot, row = k // 8 * 16, k % 8
    dt = [(row < 6) & (col == slot + 10 + row)]
    dt += [(row >= 6) & (col == slot + m * 2 + row - 6) for m in range(MODES)]
    return jnp.asarray(col == i // 10 * 16 + i % 10, BF), jnp.asarray(np.stack(dt), BF)


STEPS = 4
PER_STEP = RUNS // STEPS
ROWS_STEP = LEN // STEPS
SUBS = ROWS_STEP // SUB


def step_spec(width, back=False):
    if back:
        return pl.BlockSpec((ROWS_STEP, width), lambda i, pf: (STEPS - 1 - i, 0))
    return pl.BlockSpec((ROWS_STEP, width), lambda i, pf: (i, 0))


def pos_specs(width, back=False):
    def one(s):
        if back:
            return pl.BlockSpec((RUN, width), lambda i, pf: (pf[O_POS + (STEPS - 1 - i) * PER_STEP + s], 0))
        return pl.BlockSpec((RUN, width), lambda i, pf: (pf[O_POS + i * PER_STEP + s], 0))

    return [one(s) for s in range(PER_STEP)]


def joined(refs):
    return jnp.concatenate([ref[...] for ref in refs], axis=0)


def own_runs(s):
    return slice(s * RUN, (s + 1) * RUN)


def conv_kernel(pf, x, taps, bias, pick_x, pick_dt, w, u_out, slope_out, near, far, xw, dtw, xbuf, part_out):
    r = pl.program_id(0)

    @pl.when(r == 0)
    def _():
        last = w[:, 48:, :].reshape(256, EC)
        for m in range(MODES):
            rows = w[:, m * 16 : (m + 1) * 16, :].reshape(256, EC)
            xw[m] = nn(pick_x[...], rows).astype(BF)
            dtw[m] = (nn(pick_dt[0], rows) + nn(pick_dt[1 + m], last)).astype(BF)
        xbuf[0:8, :] = jnp.zeros((8, EC), F4)

    @pl.when(r > 0)
    def _():
        xbuf[0:8, :] = xbuf[ROWS_STEP : ROWS_STEP + 8, :]

    xbuf[8:, :] = x[...].astype(F4)
    conv = bias[...] + taps[0:1, :] * xbuf[5 : 5 + ROWS_STEP, :]
    for i in range(1, KC):
        conv = conv + taps[i : i + 1, :] * xbuf[5 + i : 5 + i + ROWS_STEP, :]
    q = jax.nn.sigmoid(conv)
    u = conv * q
    u_out[...] = u
    slope_out[...] = q * (1.0 + conv * (1.0 - q))
    u_low = u.astype(BF)
    for s in range(PER_STEP):
        part = nt(u_low[own_runs(s)], xw[pf[O_KIND + r * PER_STEP + s]])
        part_out[pl.ds(pl.multiple_of(pf[O_POS + r * PER_STEP + s] * RUN, RUN), RUN), :] = part

    @pl.when(r == STEPS - 1)
    def _():
        near[...] = part_out[: LEN // 2, :]
        far[...] = part_out[LEN // 2 :, :]


def conv_call(pf, x_pre, taps, bias, w, first):
    return pl.pallas_call(
        conv_kernel,
        out_shape=[
            jax.ShapeDtypeStruct((LEN, EC), F4),
            pltpu.HBM((LEN, EC), F4),
            jax.ShapeDtypeStruct((LEN // 2, PROJ), F4),
            jax.ShapeDtypeStruct((LEN // 2, PROJ), F4),
            jax.ShapeDtypeStruct((MODES, PROJ, EC), BF),
            jax.ShapeDtypeStruct((MODES, R, EC), BF),
        ],
        grid_spec=pltpu.PrefetchScalarGridSpec(
            num_scalar_prefetch=1,
            grid=(STEPS,),
            in_specs=[
                step_spec(EC),
                whole((KC, EC)),
                whole((1, EC)),
                whole((PROJ, 256)),
                whole((1 + MODES, R, 256)),
                pl.BlockSpec((16, TAIL_IN, EC), lambda i, pf: (0, first // TAIL_IN, 0)),
            ],
            out_specs=[
                step_spec(EC),
                step_spec(EC),
                whole((LEN // 2, PROJ)),
                whole((LEN // 2, PROJ)),
                whole((MODES, PROJ, EC)),
                whole((MODES, R, EC)),
            ],
            scratch_shapes=[
                pltpu.VMEM((ROWS_STEP + 8, EC), F4),
                pltpu.VMEM((LEN, PROJ), F4),
            ],
        ),
        compiler_params=params(14),
        cost_estimate=cost(1 << 28, 4 << 20, 1 << 20),
        name="conv_project",
    )(pf, x_pre, taps, bias, *pickers(), in_hbm(w))


def softplus(v):
    e = jnp.exp(-jnp.abs(v))
    r = 1.0 / (1.0 + e)
    return jnp.maximum(v, 0.0) + jnp.log1p(e), jnp.where(v >= 0.0, r, e * r)


def halves(v):
    high = v.astype(BF)
    return high, (v - high.astype(F4)).astype(BF)


def masks():
    col = lax.broadcasted_iota(jnp.int32, (ROWS_STEP, SUB * NS), 1)
    row = lax.broadcasted_iota(jnp.int32, (ROWS_STEP, SUB * NS), 0)
    state = lax.broadcasted_iota(jnp.int32, (NS, SUB * NS), 0)
    state_col = lax.broadcasted_iota(jnp.int32, (NS, SUB * NS), 1)
    tiled = jnp.where(state_col % NS == state, 1.0, 0.0).astype(BF)
    return col // NS == row % SUB, tiled


def diagonals(values, own, tiled, out):
    for part, v in enumerate(halves(values)):
        out[part] = jnp.where(own, nn(v, tiled), 0.0).astype(BF).reshape(SUBS, SUB, SUB * NS)


def diagonal(diag, s):
    return jnp.concatenate([diag[0, s], diag[1, s]], axis=0)


def folded(values, own, tiled):
    high, low = halves(jnp.where(own, values, 0.0))
    return nt(high, tiled) + nt(low, tiled)


def columns_of(bct, bc):
    turned = jnp.concatenate([bc, jnp.zeros((ROWS_STEP, 128 - 2 * NS), F4)], axis=1).T
    for s in range(SUBS):
        bct[s] = turned[0 : 2 * NS, s * SUB : (s + 1) * SUB]


def scan_kernel(pf, u_in, z, *refs):
    ps, refs = refs[:PER_STEP], refs[PER_STEP:]
    (dtw, dtb, rates, skip, y, gated, d_out, slope_out, marks, *scratch) = refs
    state, dbuf, wbuf, hb0, hb1, bct, diag = scratch
    r = pl.program_id(0)

    @pl.when(r == 0)
    def _():
        state[...] = jnp.zeros_like(state)

    proj = joined(ps)
    low = proj[:, :R].astype(BF)
    v = jnp.concatenate(
        [nn(low[own_runs(s)], dtw[pf[O_KIND + r * PER_STEP + s]]) for s in range(PER_STEP)], axis=0
    )
    delta, slope = softplus(v + dtb[...])
    slope_out[...] = slope
    d_out[...] = delta
    u = u_in[...]
    dbuf[...] = delta
    wbuf[...] = delta * u
    y[...] = skip[...] * u
    rate = rates[...]
    columns_of(bct, proj[:, R:])
    diagonals(proj[:, R + NS :], *masks(), diag)

    def advance(s, h, hb):
        base = pl.multiple_of(s * SUB, SUB)
        marks[s] = h
        d_rows = dbuf[pl.ds(base, SUB), :]
        w_rows = wbuf[pl.ds(base, SUB), :]
        b_cols = bct[s]
        for i in range(SUB):
            a = jnp.exp2(d_rows[i : i + 1, :] * rate)
            h = a * h + b_cols[0:NS, i : i + 1] * w_rows[i : i + 1, :]
            hb[i * NS : (i + 1) * NS, :] = h.astype(BF)
        return h

    def sums(s, hb):
        both = nn(diagonal(diag, s), hb[...])
        y[pl.ds(pl.multiple_of(s * SUB, SUB), SUB), :] += both[0:SUB] + both[SUB:]

    def pair(k, h):
        sums(2 * k, hb0)
        h = advance(2 * k + 1, h, hb1)
        sums(2 * k + 1, hb1)
        return advance(2 * k + 2, h, hb0)

    h = advance(0, state[...], hb0)
    h = lax.fori_loop(0, SUBS // 2 - 1, pair, h)
    sums(SUBS - 2, hb0)
    state[...] = advance(SUBS - 1, h, hb1)
    sums(SUBS - 1, hb1)
    zf = z[...].astype(F4)
    gated[...] = (y[...] * (zf * jax.nn.sigmoid(zf))).astype(BF)


def scan_call(pf, u, z, proj, dtw, dtb, rates, skip):
    return pl.pallas_call(
        scan_kernel,
        out_shape=[
            pltpu.HBM((LEN, EC), F4),
            jax.ShapeDtypeStruct((LEN, EC), BF),
            pltpu.HBM((LEN, EC), F4),
            pltpu.HBM((LEN, EC), F4),
            pltpu.HBM((LEN // SUB, NS, EC), F4),
        ],
        grid_spec=pltpu.PrefetchScalarGridSpec(
            num_scalar_prefetch=1,
            grid=(STEPS,),
            in_specs=[step_spec(EC), step_spec(EC)]
            + pos_specs(PROJ)
            + [whole((MODES, R, EC)), whole((1, EC)), whole((NS, EC)), whole((1, EC))],
            out_specs=[
                step_spec(EC),
                step_spec(EC),
                step_spec(EC),
                step_spec(EC),
                pl.BlockSpec((SUBS, NS, EC), lambda i, pf: (i, 0, 0)),
            ],
            scratch_shapes=[
                pltpu.VMEM((NS, EC), F4),
                pltpu.VMEM((ROWS_STEP, EC), F4),
                pltpu.VMEM((ROWS_STEP, EC), F4),
                pltpu.VMEM((SUB * NS, EC), BF),
                pltpu.VMEM((SUB * NS, EC), BF),
                pltpu.VMEM((SUBS, 2 * NS, SUB), F4),
                pltpu.VMEM((2, SUBS, SUB, SUB * NS), BF),
            ],
        ),
        compiler_params=params(20),
        cost_estimate=cost(1 << 29, 12 << 20, 9 << 20),
        name="scan_forward",
    )(pf, u, z, *[proj] * PER_STEP, dtw, dtb, rates, skip)


def back_kernel(pf, u_in, d_in, slope, gg, z, y_in, *refs):
    ps, refs = refs[:PER_STEP], refs[PER_STEP:]
    (dtw, marks, rates, skip, usg, zgrad, near, far, dt_tail, alog, dtbg, skipg, *scratch) = refs
    (carry, dtwg, hprev, gb0, rb0, pb0, pc0, gb1, rb1, pb1, pc1, *scratch) = scratch
    wbuf, ybuf, pbuf, bct, diag, cbuf, bbuf, part = scratch
    r = pl.program_id(0)

    @pl.when(r == 0)
    def _():
        carry[...] = jnp.zeros_like(carry)
        dtwg[...] = jnp.zeros_like(dtwg)
        alog[...] = jnp.zeros_like(alog)
        dtbg[...] = jnp.zeros_like(dtbg)
        skipg[...] = jnp.zeros_like(skipg)

    delta = d_in[...]
    u = u_in[...]
    zf = z[...].astype(F4)
    q = jax.nn.sigmoid(zf)
    gf = gg[...].astype(F4)
    yg = gf * (zf * q)
    zgrad[...] = (gf * y_in[...] * (q * (1.0 + zf * (1.0 - q)))).astype(BF)
    wbuf[...] = delta * u
    ybuf[...] = yg
    skipg[...] += jnp.sum(yg * u, axis=0, keepdims=True)
    rate = rates[...]
    proj = joined(ps)
    columns_of(bct, proj[:, R:])
    own, tiled = masks()
    diagonals(proj[:, R : R + NS], own, tiled, diag)

    ones = jnp.where(own[:SUB], 1.0, 0.0).astype(BF)

    def lanes(v):
        return (v[:, 0:128] + v[:, 128:256]) + (v[:, 256:384] + v[:, 384:512])

    def retreat(s, carried, bufs):
        gb, rb, pb, pc = bufs
        ag, al = carried
        base = pl.multiple_of(s * SUB, SUB)
        d_rows = d_in[pl.ds(base, SUB), :]
        w_rows = wbuf[pl.ds(base, SUB), :]
        y_rows = ybuf[pl.ds(base, SUB), :]
        bc_cols = bct[s]
        h = marks[s]
        for i in range(SUB):
            hprev[i] = h
            a = jnp.exp2(d_rows[i : i + 1, :] * rate)
            h = a * h + bc_cols[0:NS, i : i + 1] * w_rows[i : i + 1, :]
            pc[i * NS : (i + 1) * NS, :] = lanes(h * y_rows[i : i + 1, :]).astype(BF)
        for i in reversed(range(SUB)):
            g = ag + bc_cols[NS:, i : i + 1] * y_rows[i : i + 1, :]
            gb[i * NS : (i + 1) * NS, :] = g.astype(BF)
            pb[i * NS : (i + 1) * NS, :] = lanes(g * w_rows[i : i + 1, :]).astype(BF)
            ag = jnp.exp2(d_rows[i : i + 1, :] * rate) * g
            rp = rate * (ag * hprev[i])
            rb[i * NS : (i + 1) * NS, :] = rp.astype(BF)
            al = al + d_rows[i : i + 1, :] * rp
        return ag, al

    full = jnp.ones((SUB, 128), BF)

    def sums(s, bufs):
        gb, rb, pb, pc = bufs
        at = pl.ds(pl.multiple_of(s * SUB, SUB), SUB)
        both = nn(diagonal(diag, s), gb[...])
        bsum = both[0:SUB] + both[SUB:]
        dsum = nn(ones, rb[...])
        cbuf[at, :] = nt(full, pc[...])
        bbuf[at, :] = nt(full, pb[...])
        usg[at, :] = d_in[at, :] * bsum + skip[...] * ybuf[at, :]
        pbuf[at, :] = dsum * LN2 + u_in[at, :] * bsum

    even, odd = (gb0, rb0, pb0, pc0), (gb1, rb1, pb1, pc1)

    def pair(k, carried):
        s = SUBS - 1 - 2 * k
        sums(s, even)
        carried = retreat(s - 1, carried, odd)
        sums(s - 1, odd)
        return retreat(s - 2, carried, even)

    carried = retreat(SUBS - 1, (carry[...], jnp.zeros((NS, EC), F4)), even)
    carried = lax.fori_loop(0, SUBS // 2 - 1, pair, carried)
    sums(1, even)
    ag, al = retreat(0, carried, odd)
    sums(0, odd)
    carry[...] = ag
    alog[...] += al * LN2
    pre = pbuf[...] * slope[...]
    dtbg[...] += jnp.sum(pre, axis=0, keepdims=True)
    pre_low = pre.astype(BF)
    bgrad = folded(bbuf[...], own, tiled)
    cgrad = folded(cbuf[...], own, tiled)
    low = proj[:, :R].astype(BF)
    for s in range(PER_STEP):
        run = (STEPS - 1 - r) * PER_STEP + s
        kind = pf[O_KIND + run]
        at = pl.ds(pl.multiple_of(pf[O_POS + run] * RUN, RUN), RUN)
        part[at, :R] = nt(pre_low[own_runs(s)], dtw[kind])
        part[at, R : R + NS] = bgrad[own_runs(s)]
        part[at, R + NS :] = cgrad[own_runs(s)]
        dtwg[kind] += tn(low[own_runs(s)], pre_low[own_runs(s)])

    @pl.when(r == STEPS - 1)
    def _():
        near[...] = part[: LEN // 2, :]
        far[...] = part[LEN // 2 :, :]
        for s in range(16):
            for m in range(MODES):
                dt_tail[s, m * 8 : (m + 1) * 8, :] = dtwg[m, s * 8 : (s + 1) * 8, :]


def back_call(pf, u, delta, slope, gg, z, y, proj, dtw, marks, rates, skip):
    return pl.pallas_call(
        back_kernel,
        out_shape=[
            jax.ShapeDtypeStruct((LEN, EC), F4),
            jax.ShapeDtypeStruct((LEN, EC), BF),
            jax.ShapeDtypeStruct((LEN // 2, PROJ), F4),
            jax.ShapeDtypeStruct((LEN // 2, PROJ), F4),
            jax.ShapeDtypeStruct((16, MODES * 8, EC), F4),
            jax.ShapeDtypeStruct((NS, EC), F4),
            jax.ShapeDtypeStruct((1, EC), F4),
            jax.ShapeDtypeStruct((1, EC), F4),
        ],
        grid_spec=pltpu.PrefetchScalarGridSpec(
            num_scalar_prefetch=1,
            grid=(STEPS,),
            in_specs=[step_spec(EC, True)] * 6
            + pos_specs(PROJ, True)
            + [
                whole((MODES, R, EC)),
                pl.BlockSpec((SUBS, NS, EC), lambda i, pf: (STEPS - 1 - i, 0, 0)),
                whole((NS, EC)),
                whole((1, EC)),
            ],
            out_specs=[
                step_spec(EC, True),
                step_spec(EC, True),
                whole((LEN // 2, PROJ)),
                whole((LEN // 2, PROJ)),
                whole((16, MODES * 8, EC)),
                whole((NS, EC)),
                whole((1, EC)),
                whole((1, EC)),
            ],
            scratch_shapes=[
                pltpu.VMEM((NS, EC), F4),
                pltpu.VMEM((MODES, R, EC), F4),
                pltpu.VMEM((SUB, NS, EC), F4),
                *([pltpu.VMEM((SUB * NS, EC), BF)] * 2 + [pltpu.VMEM((SUB * NS, 128), BF)] * 2) * 2,
                pltpu.VMEM((ROWS_STEP, EC), F4),
                pltpu.VMEM((ROWS_STEP, EC), F4),
                pltpu.VMEM((ROWS_STEP, EC), F4),
                pltpu.VMEM((SUBS, 2 * NS, SUB), F4),
                pltpu.VMEM((2, SUBS, SUB, SUB * NS), BF),
                pltpu.VMEM((ROWS_STEP, SUB * NS), F4),
                pltpu.VMEM((ROWS_STEP, SUB * NS), F4),
                pltpu.VMEM((LEN, PROJ), F4),
            ],
        ),
        compiler_params=params(24),
        cost_estimate=cost(1 << 30, 14 << 20, 9 << 20),
        name="scan_backward",
    )(pf, u, delta, slope, gg, z, y, *[proj] * PER_STEP, dtw, marks, rates, skip)


def conv_back_kernel(pf, *refs):
    pgs, refs = refs[:PER_STEP], refs[PER_STEP:]
    (xw, usg, u, slope, x_now, x_before, taps, out, x_tail, cwg, cbg, gbuf, xbuf, xwg) = refs
    r = pl.program_id(0)

    @pl.when(r == 0)
    def _():
        xwg[...] = jnp.zeros_like(xwg)
        cwg[...] = jnp.zeros_like(cwg)
        cbg[...] = jnp.zeros_like(cbg)
        gbuf[ROWS_STEP:, :] = jnp.zeros((8, EC), F4)

    @pl.when(r > 0)
    def _():
        gbuf[ROWS_STEP:, :] = gbuf[0:8, :]

    u_low = u[...].astype(BF)
    kinds = [pf[O_KIND + (STEPS - 1 - r) * PER_STEP + s] for s in range(PER_STEP)]
    u_grad = usg[...] + jnp.concatenate([nn(pgs[s][...], xw[kinds[s]]) for s in range(PER_STEP)], axis=0)
    grad = u_grad * slope[...]
    gbuf[0:ROWS_STEP, :] = grad
    cbg[...] += jnp.sum(grad, axis=0, keepdims=True)
    before = x_before[...].astype(F4)[16 - 8 :, :]
    xbuf[0:8, :] = jnp.where(r == STEPS - 1, jnp.zeros_like(before), before)
    xbuf[8:, :] = x_now[...].astype(F4)
    back = taps[KC - 1 : KC, :] * grad
    for i in range(KC):
        cwg[i : i + 1, :] += jnp.sum(grad * xbuf[5 + i : 5 + i + ROWS_STEP, :], axis=0, keepdims=True)
        if i < KC - 1:
            back = back + taps[i : i + 1, :] * gbuf[KC - 1 - i : KC - 1 - i + ROWS_STEP, :]
    out[...] = back.astype(BF)
    for s in range(PER_STEP):
        xwg[kinds[s]] += tn(pgs[s][...], u_low[own_runs(s)])

    @pl.when(r == STEPS - 1)
    def _():
        for s in range(16):
            for m in range(MODES):
                x_tail[s, m * 10 : (m + 1) * 10, :] = xwg[m, s * 10 : (s + 1) * 10, :]
            x_tail[s, MODES * 10 :, :] = jnp.zeros((TAIL_OUT - 24 - MODES * 10, EC), F4)


def conv_back_call(pf, pg, xw, usg, u, slope, x_pre, taps):
    before = ROWS_STEP // 16
    return pl.pallas_call(
        conv_back_kernel,
        out_shape=[
            jax.ShapeDtypeStruct((LEN, EC), BF),
            jax.ShapeDtypeStruct((16, TAIL_OUT - 24, EC), F4),
            jax.ShapeDtypeStruct((KC, EC), F4),
            jax.ShapeDtypeStruct((1, EC), F4),
        ],
        grid_spec=pltpu.PrefetchScalarGridSpec(
            num_scalar_prefetch=1,
            grid=(STEPS,),
            in_specs=pos_specs(PROJ, True)
            + [
                whole((MODES, PROJ, EC)),
                step_spec(EC, True),
                step_spec(EC, True),
                step_spec(EC, True),
                step_spec(EC, True),
                pl.BlockSpec(
                    (16, EC), lambda i, pf: (jnp.maximum((STEPS - 1 - i) * before - 1, 0), 0)
                ),
                whole((KC, EC)),
            ],
            out_specs=[
                step_spec(EC, True),
                whole((16, TAIL_OUT - 24, EC)),
                whole((KC, EC)),
                whole((1, EC)),
            ],
            scratch_shapes=[
                pltpu.VMEM((ROWS_STEP + 8, EC), F4),
                pltpu.VMEM((ROWS_STEP + 8, EC), F4),
                pltpu.VMEM((MODES, PROJ, EC), F4),
            ],
        ),
        compiler_params=params(16),
        cost_estimate=cost(1 << 29, 8 << 20, 1 << 20),
        name="conv_backward",
    )(pf, *[pg] * PER_STEP, xw, usg, u, slope, x_pre, x_pre, taps)


def ring(v, axis, step):
    return lax.ppermute(v, axis, [(i, (i + step) % 4) for i in range(4)])


def across(v):
    return lax.ppermute(v, "c", [(0, 1), (1, 0)])


def after(value, *others):
    return lax.optimization_barrier((value, others))[0]


def add(*values):
    total = values[0].astype(F4)
    for value in values[1:]:
        total = total + value.astype(F4)
    return total


def spread_chan(rows):
    left = ring(rows, "y", 1)
    right = ring(rows, "y", -1)
    far = [ring(left[:RUN], "y", 1), ring(right[RUN:], "y", -1)]
    near = jnp.concatenate([rows, right, *far, left], axis=0)
    return jnp.concatenate([near, across(near)], axis=0)


def collect_chan(near, far):
    pair = add(near, across(far)).astype(BF).reshape(4, 2 * RUN, D)
    own, right, far_first, far_second, left = pair[0], pair[1], pair[2, :RUN], pair[2, RUN:], pair[3]
    came = ring(far_first, "y", 1)
    came_back = ring(far_second, "y", -1)
    right = jnp.concatenate([add(right[:RUN], came).astype(BF), right[RUN:]], axis=0)
    left = jnp.concatenate([left[:RUN], add(left[RUN:], came_back).astype(BF)], axis=0)
    return add(own, ring(right, "y", 1), ring(left, "y", -1))


def direct(v, axis):
    return [v, ring(v, axis, -1), ring(v, axis, 2), ring(v, axis, 1)]


def sum_chan(near, far, finish, fill=None):
    pair = add(near, across(far)).reshape(4, LEN // 8, near.shape[1])
    came = [ring(pair[1], "y", 1), ring(pair[2], "y", 2), ring(pair[3], "y", -1)]
    filled = None
    if fill:
        filled = fill(pair)
        came = after(came, filled)
    mine = jnp.concatenate(direct(finish(add(pair[0], *came)), "y"), axis=0)
    return jnp.concatenate([mine, across(mine)], axis=0), filled


def sum_axis(v, axis):
    v = jnp.roll(v, -lax.axis_index(axis), 0)
    return add(v[0], ring(v[1], axis, 1), ring(v[2], axis, 2), ring(v[3], axis, -1))


def sum_pair(v):
    place = lax.axis_index("c")
    keep = lax.dynamic_index_in_dim(v, place, 2, False)
    give = lax.dynamic_index_in_dim(v, 1 - place, 2, False)
    return sum_axis(jnp.swapaxes(keep + across(give), 0, 1), "y")


def sum_seq(v):
    return sum_axis(sum_axis(v.reshape(4, 4, v.shape[1]), "z"), "x")


def local(
    layer_input, kinds, norm_gain, in_weight, conv_weight, conv_bias, x_weight, dt_weight,
    dt_bias, a_log, d_skip, out_weight, cotangent,
):
    place_y, place_c = lax.axis_index("y"), lax.axis_index("c")
    chan = place_y * 2 + place_c
    gain = norm_gain.astype(F4)
    taps = conv_weight.astype(F4)
    cbias = conv_bias.astype(F4)[None, :]
    dtb = dt_bias.astype(F4)[None, :]
    a_own = lax.dynamic_slice_in_dim(a_log, chan * EC, EC, 1).astype(F4)
    rates = -jnp.exp(a_own) * LOG2E
    skip = lax.dynamic_slice_in_dim(d_skip, chan * EC, EC, 0).astype(F4)[None, :]

    x32 = layer_input.astype(F4)
    rms = lax.rsqrt(jnp.mean(x32 * x32, axis=1, keepdims=True) + 1e-05)
    normed = (x32 * rms * gain[None, :]).astype(BF)

    early_w = lax.all_gather(
        jnp.concatenate(
            [
                in_weight[:, :, 0, :].reshape(ROWS, EC),
                in_weight[:, :, 1, :].reshape(ROWS, EC),
                jnp.concatenate([x_weight, dt_weight[:, :6]], axis=1).reshape(48, EC),
                jnp.pad(dt_weight[:, 6:].reshape(6, EC), ((0, 10), (0, 0))),
            ],
            axis=0,
        ),
        SEQ,
    )
    pf = slot_plan(kinds)
    xs = spread_chan(normed)
    cs = spread_chan(cotangent)
    out_w = lax.all_gather(after(out_weight.reshape(ROWS, EC), xs, cs), SEQ)
    rates, skip, taps, cbias, dtb, xs = after((rates, skip, taps, cbias, dtb, xs), pf)
    early_w = after(early_w, rates, skip, taps, cbias, dtb, xs)
    x_pre = down(pf, in_hbm(xs), early_w, "project_scan")
    u, conv_slope, near, far, xw, dtw = conv_call(pf, x_pre, taps, cbias, early_w, 2 * ROWS)
    proj, z = sum_chan(
        near,
        far,
        lambda total: total,
        lambda pair: down(after(pf, pair), xs, early_w, "project_gate", MODES),
    )
    y, gated, delta, slope, marks = scan_call(pf, u, z, proj, dtw, dtb, rates, skip)

    out_part = outer(pf, "out_weight_grad", cs, gated, ROWS)
    out_sum = lax.psum_scatter(out_part, SEQ, scatter_dimension=0).astype(F4)
    gg = down(after(pf, out_part), in_hbm(cs), out_w, "project_cotangent")
    usg, zgrad, near, far, dt_tail, alog, dtbg, skipg = back_call(
        pf, u, delta, slope, gg, z, y, proj, dtw, marks, rates, skip
    )
    pg, weights_part = sum_chan(
        near,
        far,
        lambda total: total.astype(BF),
        lambda pair: outer(after(pf, pair), "gate_weight_grad", xs, zgrad, 2 * ROWS + TAIL_OUT),
    )
    xgrad, x_tail, cwg, cbg = conv_back_call(pf, pg, xw, usg, u, conv_slope, x_pre, taps)
    weights_part = outer(
        after(pf, out_sum),
        "scan_weight_grad",
        xs,
        xgrad,
        2 * ROWS + TAIL_OUT,
        ROWS,
        weights_part,
        (dt_tail, x_tail),
    )
    in_grad, x_w_grad, dt_w_grad = unpack(lax.psum_scatter(weights_part, SEQ, scatter_dimension=0))

    pf = after(pf, weights_part)
    branch = collect_chan(*up(pf, "project_out", (gated, out_w, 0)))
    mixed = (x32 + branch).astype(BF)
    near, far, gain_part = up(
        pf, "input_grad", (xgrad, early_w, 0), (zgrad, early_w, MODES), xs=xs
    )
    ngrad = collect_chan(near, far) * gain[None, :]
    x_grad = (
        cotangent.astype(F4)
        + rms * ngrad
        - x32 * (rms * rms * rms) * jnp.mean(ngrad * x32, axis=1, keepdims=True)
    )
    out_grad = out_sum.reshape(MODES, 128, EC)
    gain_part = sum_pair((gain_part[0] / gain).reshape(16, 4, 2, 16))
    small = jnp.concatenate([cwg, cbg, dtbg, skipg, alog], axis=0)
    small = jnp.swapaxes(small.reshape(23, 16, 32), 0, 1).reshape(16, 23 * 32)
    small = sum_seq(jnp.concatenate([small, gain_part, jnp.zeros((16, 16), F4)], axis=1))
    gain_grad = small[23 * 32 : 24 * 32 - 16]
    moves = [(s * 8 + c, c * 16 + s) for s in range(16) for c in range(8)]
    own = lax.ppermute(small[: 23 * 32].reshape(23, 32), ("z", "x", "y", "c"), moves)
    return (
        mixed,
        x_grad,
        gain_grad,
        in_grad,
        own[0:4],
        own[4],
        x_w_grad,
        dt_w_grad,
        own[5],
        own[7:],
        own[6],
        out_grad,
    )


def solution(mesh):
    fine = Mesh(mesh.devices.reshape(4, 4, 4, 2), ("z", "x", "y", "c"))
    rows = ("z", "x", "y", "c")
    return jax.shard_map(
        local,
        mesh=fine,
        in_specs=(
            P(rows, None),
            P(SEQ),
            P(),
            P(None, SEQ, None, CHAN),
            P(None, CHAN),
            P(CHAN),
            P(None, SEQ, CHAN),
            P(None, SEQ, CHAN),
            P(CHAN),
            P(),
            P(),
            P(None, SEQ, CHAN),
            P(rows, None),
        ),
        out_specs=(
            P(rows, None),
            P(rows, None),
            P(rows),
            P(None, SEQ, None, CHAN),
            P(None, rows),
            P(rows),
            P(None, SEQ, CHAN),
            P(None, SEQ, CHAN),
            P(rows),
            P(None, rows),
            P(rows),
            P(None, SEQ, CHAN),
        ),
        check_vma=False,
    )
```
